256 devices in a mesh: grp: 2 (over core), ep: 128 (over y, x, z).
Axes of the slice: x: 4, y: 4, z: 8, core: 2. Of those that a mesh axis runs over, the one named last changes fastest.
Arguments:
- hidden: bfloat16 [2, 32768, 2048], P('grp', 'ep'), may hold values from -6 to 6
- norm_gain: float32 [2, 2048], P('grp'), may hold values from 0.1 to 1.9
- final_gain: float32 [2, 2048], P('grp'), may hold values from 0.1 to 1.9
- router: bfloat16 [2, 2048, 128], P('grp'), may hold values from -0.125 to 0.125
- w_in: bfloat16 [2, 2048, 131072], P('grp', None, 'ep'), may hold values from -0.125 to 0.125
- w_out: bfloat16 [2, 131072, 2048], P('grp', 'ep'), may hold values from -0.375 to 0.375
- expert_ids: int32 [2, 32768, 2], P('grp', 'ep'), may hold values from 0 to 127, as said below
- slot_ids: int32 [2, 32768, 2], P('grp', 'ep'), may hold values from -1 to 5, as said below
- src_len: int32 [128, 4], P('ep'), may hold values from 1 to 128, 256 in all within a row
- tgt_len: int32 [128, 4], P('ep'), may hold values from 1 to 85, 171 in all within a row
- wq: bfloat16 [2048, 1024], P('ep'), may hold values from -1 to 1
- wk: bfloat16 [2048, 1024], P('ep'), may hold values from -1 to 1
- wv: bfloat16 [2048, 1024], P('ep'), may hold values from -0.125 to 0.125
- wo: bfloat16 [2048, 1024], P('ep'), may hold values from -0.5 to 0.5
Outputs:
- layer_out: bfloat16 [2, 32768, 2048], P('grp', 'ep')
The draws below stay inside these ranges and needn't reach their ends.
Inputs may be any that keep to these rules, and one draw needn't show every extreme that they name: `expert_ids`: each row names two different experts; at most one of them is below 16. `slot_ids`: -1 where the expert is 16 or more; otherwise a slot that no other route of the same device block to the same expert takes. In each group one expert gets all 6 slots from every device block.
All inputs are finite; a program needn't handle non-finite values.
Results may differ from the reference program's by a relative error of at most 0.02.
The reference program's roundings to bfloat16 on the way count: a program that leaves them out, or rounds other values in their place, can miss the bound.
Values may be sent and summed in bfloat16 or wider, within the bound.
A program may use at most 128 MiB of HBM per device.

```python
import math
import jax
import jax.numpy as jnp
import numpy as np
from jax import lax

D = 2048
FF = 8192
EXPERTS = 128
HEADS = 8
HD = 128
SPLIT = 8
C = 6
ROWS = 256
SENT = 4
E_WIN = 16
FF_DEV = 1024
HW = 1024
TOKENS = 32768
SRC_MOST = 128
TGT_TOTAL = 171
TGT_MOST = 85
N_EP = 128


def route_tables(key):
    blocks = 2 * N_EP
    k_hot, k_dev, k_cnt, k_perm, k_side, k_first, k_second = jax.random.split(key, 7)
    hot_group = jnp.repeat(jax.random.randint(k_hot, (2, 1), 0, E_WIN), N_EP, axis=0)
    hot_dev = jax.random.randint(k_dev, (blocks, 1), 0, E_WIN)
    expert_iota = jnp.arange(E_WIN, dtype=jnp.int32)[None, :]
    counts = jax.random.randint(k_cnt, (blocks, E_WIN), (C + 2) // 3, C + 1)
    counts = jnp.where((expert_iota == hot_group) | (expert_iota == hot_dev), C, counts)
    order = jnp.arange(ROWS, dtype=jnp.int32)
    q_expert = jnp.minimum(order // C, E_WIN - 1)
    q_slot = order % C
    fill = jnp.take_along_axis(counts, jnp.broadcast_to(q_expert[None, :], (blocks, ROWS)), axis=1)
    live = (order[None, :] < E_WIN * C) & (q_slot[None, :] < fill)
    expert_q = jnp.where(live, q_expert[None, :], -1)
    slot_q = jnp.where(live, q_slot[None, :], -1)
    perms = jax.vmap(lambda k: jax.random.permutation(k, ROWS))(jax.random.split(k_perm, blocks))
    block_iota = jnp.arange(blocks, dtype=jnp.int32)[:, None]
    win_expert = jnp.zeros((blocks, ROWS), jnp.int32).at[block_iota, perms].set(expert_q)
    win_slot = jnp.zeros((blocks, ROWS), jnp.int32).at[block_iota, perms].set(slot_q)
    span = EXPERTS - E_WIN
    first = E_WIN + jax.random.randint(k_first, (blocks, ROWS), 0, span)
    second = E_WIN + (first - E_WIN + 1 + jax.random.randint(k_second, (blocks, ROWS), 0, span - 1)) % span
    has = win_expert >= 0
    lead = jnp.where(has, win_expert, first)
    other = jnp.where(has, first, second)
    slot_lead = jnp.where(has, win_slot, -1)
    side = jax.random.randint(k_side, (blocks, ROWS), 0, 2)
    id_zero = jnp.where(side == 1, other, lead)
    id_one = jnp.where(side == 1, lead, other)
    slot_zero = jnp.where(side == 1, -1, slot_lead)
    slot_one = jnp.where(side == 1, slot_lead, -1)
    ids = jnp.stack([id_zero, id_one], axis=-1).reshape(2, TOKENS, 2).astype(jnp.int32)
    slots = jnp.stack([slot_zero, slot_one], axis=-1).reshape(2, TOKENS, 2).astype(jnp.int32)
    return (ids, slots)


def draw_expert_ids(key, part):
    return route_tables(key)[0]


def draw_slot_ids(key, part):
    return route_tables(key)[1]


def draw_wq(key, part):
    key = jax.random.fold_in(key, 21)
    own = jax.random.normal(key, (D, HW), jnp.float32)
    values = own * D ** (-0.5)
    return jnp.clip(values, -1.0, 1.0).astype(jnp.bfloat16)


def draw_wk(key, part):
    key = jax.random.fold_in(key, 22)
    own = jax.random.normal(key, (D, HW), jnp.float32)
    values = own * D ** (-0.5)
    return jnp.clip(values, -1.0, 1.0).astype(jnp.bfloat16)


def spiked(drawn, rng, source, target, blocks, factor):
    owner, partner = [(jnp.arange(drawn.shape[dim]) // (drawn.shape[dim] // blocks)).reshape([-1 if axis == dim else 1 for axis in range(drawn.ndim)]) for dim in (source, target)]
    chosen = jax.random.permutation(rng, blocks)[partner]
    strong = (owner == chosen) | (owner == (partner + blocks // 2) % blocks)
    return jnp.where(strong, factor * drawn, drawn)


def levels(rng, shape, cuts, low, top_value):
    level = 1.0
    for dim, blocks in cuts:
        heights = jax.random.uniform(jax.random.fold_in(jax.random.fold_in(rng, 6), dim), (blocks,), jnp.float32, low / len(cuts), top_value / len(cuts))
        level = level * jnp.repeat(jnp.exp(heights), shape[dim] // blocks).reshape((-1,) + (1,) * (len(shape) - 1 - dim))
    return level


def split_up(number_of, total, bound, slope):
    loads = [(1 << 20) // math.isqrt(standing ** slope) + 1 for standing in range(2, number_of + 1)]
    rest, given = total - bound - (number_of - 1), [1] * (number_of - 1)
    while rest > 0:
        movable = [i for i in range(number_of - 1) if given[i] < bound]
        whole, remaining = sum([loads[i] for i in movable]), rest
        for i in movable:
            more = min(bound - given[i], max(1, remaining * loads[i] // whole), rest)
            given[i] = given[i] + more
            rest = rest - more
    return np.array([bound] + given)


def ragged_sizes(rng, amount, total, reach, skew):
    if amount == 2:
        one = jax.random.randint(rng, (), max(1, total - reach), min(reach, total - 1) + 1)
        return jnp.stack([one, total - one])
    sizes = jnp.asarray(split_up(amount, total, reach, skew), jnp.int32)
    pairs = (amount - 1) // 2
    giver, receiver = sizes[1:1 + 2 * pairs:2], sizes[2:2 + 2 * pairs:2]
    margin = jnp.minimum(giver - 1, reach - receiver)
    shifted = jax.random.randint(jax.random.fold_in(rng, 1), (pairs,), 0, 1 << 20) % (margin + 1)
    sizes = sizes.at[1:1 + 2 * pairs:2].set(giver - shifted).at[2:2 + 2 * pairs:2].set(receiver + shifted)
    return sizes[jax.random.permutation(jax.random.fold_in(rng, 2), amount)]


def scatter_about(stream_key, shape, width, most, cuts=(), kind=jnp.bfloat16):
    result = width * jax.random.normal(stream_key, shape, jnp.float32)
    if cuts:
        result = result * levels(stream_key, shape, cuts, -0.22, 0.18)
    return jnp.clip(result, -most, most).astype(kind)


def heavy_noise(rng, extent, deviation, most, cuts, heavy, kind=jnp.bfloat16):
    result = deviation * jax.random.normal(rng, extent, jnp.float32)
    if cuts:
        result = result * levels(rng, extent, cuts, -0.22, 0.18)
    return jnp.clip(spiked(result, jax.random.fold_in(rng, 3), *heavy), -most, most).astype(kind)


def setup_inputs(seed: int = 0) -> dict:
    key_of = jax.random.split(jax.random.key(seed), 15)
    hidden = scatter_about(key_of[0], (2, TOKENS, D), 1.0, 6.0, ((0, 2), (1, 128)))
    norm_gain = jnp.clip(1.0 + 0.18 * jax.random.normal(key_of[1], (2, D), jnp.float32), 0.1, 1.9)
    final_gain = jnp.clip(1.0 + 0.18 * jax.random.normal(key_of[2], (2, D), jnp.float32), 0.1, 1.9)
    router = scatter_about(key_of[3], (2, D, EXPERTS), D ** -0.5, 0.125, ((0, 2),))
    w_in = scatter_about(key_of[4], (2, D, E_WIN * FF), D ** -0.5, 0.125, ((0, 2), (2, 128)))
    w_out = heavy_noise(key_of[5], (2, E_WIN * FF, D), (FF // 2) ** -0.5, 0.375, ((0, 2), (1, 128)), (1, 2, 128, 5.5))
    expert_ids = draw_expert_ids(jax.random.fold_in(key_of[14], 71), 0)
    slot_ids = draw_slot_ids(jax.random.fold_in(key_of[14], 71), 0)
    src_len = jax.vmap(lambda own: ragged_sizes(own, SENT, ROWS, SRC_MOST, 2))(jax.random.split(key_of[8], N_EP)).reshape((N_EP, SENT)).astype(jnp.int32)
    tgt_len = jax.vmap(lambda own: ragged_sizes(own, SENT, TGT_TOTAL, TGT_MOST, 2))(jax.random.split(key_of[9], N_EP)).reshape((N_EP, SENT)).astype(jnp.int32)
    wq = draw_wq(jax.random.fold_in(key_of[14], 71), 0)
    wk = draw_wk(jax.random.fold_in(key_of[14], 71), 0)
    wv = scatter_about(key_of[12], (D, HW), D ** -0.5, 0.125, ((0, 128),))
    wo = scatter_about(key_of[13], (D, HW), (HW // 8) ** -0.5, 0.5, ((0, 128),))
    return dict(hidden=hidden, norm_gain=norm_gain, final_gain=final_gain, router=router, w_in=w_in, w_out=w_out, expert_ids=expert_ids, slot_ids=slot_ids, src_len=src_len, tgt_len=tgt_len, wq=wq, wk=wk, wv=wv, wo=wo)


def layer_norm(values, gain):
    mean = lax.optimization_barrier(jnp.mean(values, -1, keepdims=True))
    centred = values - mean
    spread = lax.optimization_barrier(jnp.mean(centred * centred, -1, keepdims=True))
    return centred * lax.rsqrt(spread + 1e-05) * gain

def segments(lengths, count):
    ends = jnp.cumsum(lengths).astype(jnp.int32)
    above = (jnp.arange(count, dtype=jnp.int32)[:, None] >= ends[None, :]).astype(jnp.int32)
    return lax.optimization_barrier(jnp.sum(above, axis=1)).astype(jnp.int32)

def group_moe(hidden, norm_gain, router, w_in, w_out, expert_ids, slot_ids):
    resid = hidden.astype(jnp.float32)
    normed = layer_norm(resid, norm_gain).astype(jnp.bfloat16)
    logits = jnp.dot(normed, router, preferred_element_type=jnp.float32)
    picked = jnp.take_along_axis(logits, expert_ids, axis=1)
    gate = jax.nn.sigmoid(picked - picked[:, ::-1])
    live = slot_ids >= 0
    place = lax.optimization_barrier(jnp.max(jnp.where(live, expert_ids * C + slot_ids, -1), axis=1)).astype(jnp.int32)
    weight = lax.optimization_barrier(jnp.sum(jnp.where(live, gate, jnp.float32(0.0)), axis=1))
    place_dev = place.reshape(N_EP, ROWS)
    normed_dev = normed.reshape(N_EP, ROWS, D)
    slots_all = E_WIN * C

    def pack(args):
        spots, rows = args
        target = jnp.where(spots >= 0, spots, slots_all).astype(jnp.int32)
        buffer = jnp.zeros((slots_all + 1, D), jnp.bfloat16).at[target].set(rows)
        return buffer[:slots_all]
    packed = lax.map(pack, (place_dev, normed_dev)).reshape(N_EP, E_WIN, C, D)

    def expert(index):
        rows = lax.dynamic_index_in_dim(packed, index, 1, keepdims=False).reshape(N_EP * C, D)
        first = lax.dynamic_slice_in_dim(w_in, index * FF, FF, 1)
        second = lax.dynamic_slice_in_dim(w_out, index * FF, FF, 0)
        inner = jax.nn.relu(jnp.dot(rows, first, preferred_element_type=jnp.float32)).astype(jnp.bfloat16)
        total = jnp.zeros((N_EP * C, D), jnp.float32)
        for piece_index in range(SPLIT):
            low = piece_index * FF_DEV
            part = jnp.dot(inner[:, low:low + FF_DEV], second[low:low + FF_DEV], preferred_element_type=jnp.float32)
            part = lax.optimization_barrier(part.astype(jnp.bfloat16))
            total = total + part.astype(jnp.float32)
        return total.reshape(N_EP, C, D)
    outputs = lax.map(expert, jnp.arange(E_WIN, dtype=jnp.int32))
    combined = jnp.transpose(outputs, (1, 0, 2, 3)).reshape(N_EP, E_WIN * C, D)

    def unpack(args):
        table, spots = args
        return jnp.take(table, jnp.maximum(spots, 0), axis=0)
    moe_rows = lax.map(unpack, (combined, place_dev)).reshape(TOKENS, D)
    return resid + moe_rows * weight[:, None]

def reference(hidden, norm_gain, final_gain, router, w_in, w_out, expert_ids, slot_ids, src_len, tgt_len, wq, wk, wv, wo):
    mixed = [group_moe(hidden[g], norm_gain[g], router[g], w_in[g], w_out[g], expert_ids[g], slot_ids[g]) for g in range(2)]
    normed_out = [layer_norm(mixed[g], final_gain[g]).astype(jnp.bfloat16) for g in range(2)]
    memory = normed_out[0]
    query = jnp.dot(normed_out[1], wq, preferred_element_type=jnp.float32).astype(jnp.bfloat16)
    keys = jnp.dot(memory, wk, preferred_element_type=jnp.float32).astype(jnp.bfloat16)
    values = jnp.dot(memory, wv, preferred_element_type=jnp.float32).astype(jnp.bfloat16)
    query = query.reshape(N_EP, ROWS, HEADS, HD)
    keys = keys.reshape(N_EP, ROWS, HEADS, HD)
    values = values.reshape(N_EP, ROWS, HEADS, HD)

    def attend(args):
        block_q, block_k, block_v, lengths_t, lengths_s = args
        seg_q = segments(lengths_t, ROWS)
        seg_k = segments(lengths_s, ROWS)
        valid = seg_q < SENT
        allowed = (seg_q[:, None] == seg_k[None, :]) & valid[:, None]
        scores = jnp.einsum('qhd,khd->hqk', block_q.astype(jnp.float32), block_k.astype(jnp.float32)) * HD ** (-0.5)
        scores = jnp.where(allowed[None], scores, jnp.float32(-1e+30))
        top = lax.optimization_barrier(jnp.max(scores, axis=-1, keepdims=True))
        expd = jnp.exp(scores - top)
        prob = (expd / lax.optimization_barrier(jnp.sum(expd, axis=-1, keepdims=True))).astype(jnp.bfloat16)
        context = jnp.einsum('hqk,khd->qhd', prob.astype(jnp.float32), block_v.astype(jnp.float32))
        context = context.astype(jnp.bfloat16).reshape(ROWS, HW)
        out = jnp.dot(context, wo.T, preferred_element_type=jnp.float32)
        return jnp.where(valid[:, None], out, jnp.float32(0.0))
    attended = lax.map(attend, (query, keys, values, tgt_len, src_len)).reshape(TOKENS, D)
    decoded = (mixed[1] + attended).astype(jnp.bfloat16)
    return jnp.stack([memory, decoded])
```

```python
import jax
import jax.numpy as jnp
from jax import lax
from jax.experimental import pallas as pl
from jax.experimental.pallas import tpu as pltpu
from jax.sharding import PartitionSpec as P

NY, NX, NZ = 4, 4, 8
E = NY * NX
C = 6
HALF = E // 2 * C
SENT = 4
HD = 128
ROWS_Q = 176
F32 = jnp.float32
BF16 = jnp.bfloat16

UP_ORDER = [(0, 1), (1, 1), (0, 2), (1, 2), (0, 3), (1, 3), (0, 4)]
DOWN_ORDER = [(1, 1), (0, 1), (1, 2), (0, 2), (1, 3), (0, 3), (1, 4)]
BACK_DOWN = [(1, 3), (0, 4), (1, 2), (0, 3), (1, 1), (0, 2), (0, 1)]
BACK_UP = [(0, 3), (1, 4), (0, 2), (1, 3), (0, 1), (1, 2), (1, 1)]
FAR_DOWN = (4, 3)
FAR_UP = (3, 4)


def back_slot(far, half, k):
    return (far[0] if half else 0) + k


def norm_rows(v, gain):
    mean = jnp.mean(v, -1, keepdims=True)
    centred = v - mean
    spread = jnp.mean(centred * centred, -1, keepdims=True)
    return centred * lax.rsqrt(spread + 1e-05) * gain


def kernel(
    hidden_hbm, norm_gain, final_gain, router_hbm, w_in_hbm, w_out_hbm, ids_ref, slots_ref, src_ref, tgt_ref,
    wq_ref, wk_ref, wv_ref, wo_ref,
    out_ref,
    hid, normed, router, w_in, w_out, packed, arrived, tokens, partial, sums, inner, total, returning, returned,
    mixed, weights, kv_out, kv_in, query, context, gate_ref, place_ref,
    load_sem, pack_send, pack_recv, ring_send, ring_recv, back_send, back_recv, wz_send, wz_recv,
    wxy_send, wxy_recv, ret_send, ret_recv, kv_send, kv_recv,
):
    rows, width = hid.shape
    hw = width // 2
    ep = lax.axis_index("ep")
    grp = lax.axis_index("grp")
    z = lax.rem(ep, NZ)
    e = ep // NZ
    x = lax.rem(e, NX)
    y = e // NX

    def at(yy, xx, zz):
        return (yy * NX + xx) * NZ + zz

    def zmod(v):
        return lax.rem(v + NZ, NZ)

    def xmod(v):
        return lax.rem(v + NX, NX)

    def remote(src, dst, send, recv, target):
        return pltpu.make_async_remote_copy(
            src_ref=src, dst_ref=dst, send_sem=send, recv_sem=recv,
            device_id={"ep": target}, device_id_type=pl.DeviceIdType.MESH,
        )

    sent = []

    def send(*args):
        copy = remote(*args)
        copy.start()
        sent.append(copy)

    def landed(dst, recv):
        remote(dst, dst, kv_send.at[0], recv, ep).wait_recv()

    z_up, z_down = at(y, x, zmod(z + 1)), at(y, x, zmod(z - 1))
    peers = []
    for dy in (2, 1, 3, 0):
        for dx in (2, 1, 3, 0):
            if dy or dx:
                peers.append((xmod(y + dy), xmod(x + dx)))

    loads = [
        pltpu.make_async_copy(hidden_hbm, hid, load_sem.at[0]),
        pltpu.make_async_copy(router_hbm, router, load_sem.at[1]),
        pltpu.make_async_copy(w_in_hbm, w_in, load_sem.at[2]),
        pltpu.make_async_copy(w_out_hbm, w_out, load_sem.at[3]),
    ]
    loads[0].start()
    barrier = pltpu.get_barrier_semaphore()
    for target in [at(yy, xx, z) for yy, xx in peers] + [z_up, z_down]:
        pl.semaphore_signal(barrier, inc=1, device_id={"ep": target}, device_id_type=pl.DeviceIdType.MESH)
    pl.semaphore_signal(barrier, inc=1, device_id={"grp": 1 - grp}, device_id_type=pl.DeviceIdType.MESH)
    for copy in loads[1:]:
        copy.start()

    first = grp == 0
    weights[0, e, z] = jnp.where(first, wk_ref[...], wq_ref[...])
    weights[1, e, z] = jnp.where(first, wv_ref[...], wo_ref[...])

    ids_row = ids_ref[...]
    slots_row = slots_ref[...]
    place_row = jnp.max(jnp.where(slots_row >= 0, ids_row * 16 + slots_row, -1000), axis=0, keepdims=True)
    stacked = jnp.concatenate([ids_row, slots_row, jnp.broadcast_to(place_row, (4, rows))], axis=0)
    columns = jnp.transpose(stacked.astype(F32)).astype(jnp.int32)
    ids, live = columns[:, 0:2], columns[:, 2:4] >= 0
    place_ref[...] = columns[:, 4:5]

    loads[0].wait()

    def norm_in(i, carry):
        at_rows = pl.ds(pl.multiple_of(i * 32, 32), 32)
        normed[at_rows, :] = norm_rows(hid[at_rows, :].astype(F32), norm_gain[...]).astype(BF16)
        return carry

    lax.fori_loop(0, rows // 32, norm_in, 0)

    slot_iota = lax.broadcasted_iota(jnp.int32, (E * 16, rows), 0)
    pick0 = (slot_iota == place_row).astype(F32).astype(BF16)
    pick1 = (slot_iota == place_row + 8).astype(F32).astype(BF16)
    for j in range(hw // 256):
        c0, c1 = j * 256, hw + j * 256
        got = jnp.dot(pick0, normed[:, c0:c0 + 256], preferred_element_type=F32) + jnp.dot(
            pick1, normed[:, c1:c1 + 256], preferred_element_type=F32
        )
        packed[:, :, c0:c0 + 256] = got.astype(BF16).reshape(E, 16, 256)

    pl.semaphore_wait(barrier, len(peers) + 3)

    for i, (yy, xx) in enumerate(peers):
        peer = yy * NX + xx
        send(packed.at[peer], arrived.at[e], pack_send.at[i], pack_recv.at[e], peer * NZ + z)
    own = pltpu.make_async_copy(packed.at[e], arrived.at[e], load_sem.at[4])
    own.start()

    def wz_hop(slot):
        for way, (order, sign, target) in enumerate(((UP_ORDER, 1, z_up), (DOWN_ORDER, -1, z_down))):
            half, k = order[slot]
            block = zmod(z - sign * (k - 1))
            ref = weights.at[half, e, block]
            send(ref, ref, wz_send.at[way, slot], wz_recv.at[way, slot], target)

    def wz_wait(slot):
        for way, (order, sign) in enumerate(((UP_ORDER, 1), (DOWN_ORDER, -1))):
            half, k = order[slot]
            ref = weights.at[half, e, zmod(z - sign * k)]
            landed(ref, wz_recv.at[way, slot])

    wz_hop(0)
    wz_hop(1)

    loads[1].wait()
    logits = jnp.dot(normed[...], router[...], preferred_element_type=F32)
    lane = lax.broadcasted_iota(jnp.int32, logits.shape, 1)
    pick_a = jnp.sum(jnp.where(lane == ids[:, 0:1], logits, 0.0), axis=1, keepdims=True)
    pick_b = jnp.sum(jnp.where(lane == ids[:, 1:2], logits, 0.0), axis=1, keepdims=True)
    gate_ref[...] = jnp.where(live[:, 0:1], jax.nn.sigmoid(pick_a - pick_b), 0.0) + jnp.where(
        live[:, 1:2], jax.nn.sigmoid(pick_b - pick_a), 0.0
    )

    for slot in range(5):
        wz_wait(slot)
        wz_hop(slot + 2)

    own.wait()
    for yy, xx in peers:
        peer = yy * NX + xx
        landed(arrived.at[peer], pack_recv.at[peer])
    r_iota = lax.broadcasted_iota(jnp.int32, (HALF, E * 8), 0)
    q_iota = lax.broadcasted_iota(jnp.int32, (HALF, E * 8), 1)
    base = (r_iota // C) * 16 + r_iota % C
    fold0 = (q_iota == base).astype(F32).astype(BF16)
    fold1 = (q_iota == base + 8).astype(F32).astype(BF16)
    for half in range(2):
        got = arrived[half * (E // 2):(half + 1) * (E // 2)].reshape(E * 8, hw)
        tokens[z, half, :, :hw] = jnp.dot(fold0, got, preferred_element_type=F32).astype(BF16)
        tokens[z, half, :, hw:] = jnp.dot(fold1, got, preferred_element_type=F32).astype(BF16)

    def ring_hop(slot):
        for way, (order, sign, target) in enumerate(((UP_ORDER, 1, z_up), (DOWN_ORDER, -1, z_down))):
            half, k = order[slot]
            ref = tokens.at[zmod(z - sign * (k - 1)), half]
            send(ref, ref, ring_send.at[way, slot], ring_recv.at[way, slot], target)

    def ring_wait(slot):
        for way, (order, sign) in enumerate(((UP_ORDER, 1), (DOWN_ORDER, -1))):
            half, k = order[slot]
            landed(tokens.at[zmod(z - sign * k), half], ring_recv.at[way, slot])

    def expert(block_a, half_a, block_b, half_b):
        def first_step(j, carry):
            cols = pl.ds(pl.multiple_of(j * 256, 256), 256)
            both = jnp.concatenate([tokens[block_a, half_a], tokens[block_b, half_b]], axis=0)
            got = jnp.dot(both, w_in[:, cols], preferred_element_type=F32)
            inner[:, cols] = jnp.maximum(got, 0.0).astype(BF16)
            return carry

        def second_step(j, carry):
            cols = pl.ds(pl.multiple_of(j * 256, 256), 256)
            got = jnp.dot(inner[...], w_out[:, cols], preferred_element_type=F32).astype(BF16)
            partial[block_a, half_a, :, cols] = got[:HALF]
            partial[block_b, half_b, :, cols] = got[HALF:]
            return carry

        lax.fori_loop(0, w_in.shape[1] // 256, first_step, 0)
        lax.fori_loop(0, width // 256, second_step, 0)

    def expert_slot(slot):
        (half_a, k), (half_b, _) = UP_ORDER[slot], DOWN_ORDER[slot]
        expert(zmod(z - k), half_a, zmod(z + k), half_b)

    def block_at(w, a, b):
        xx, yy = (xmod(x + a), xmod(y + b)) if w == 0 else (xmod(x + b), xmod(y + a))
        return yy * NX + xx

    def go(w, phase, sign):
        if (w == 0) == (phase == 0):
            return at(y, xmod(x + sign), z)
        return at(xmod(y + sign), x, z)

    w_count = [0]

    def wxy(w, a, b, part, phase, sign):
        blk = block_at(w, a, b)
        ref = weights.at[w, blk] if part is None else weights.at[w, blk, pl.ds(part * 4, 4)]
        send(ref, ref, wxy_send.at[w_count[0]], wxy_recv.at[w, blk, part or 0], go(w, phase, sign))
        w_count[0] += 1

    def wxy_wait(w, a, b):
        blk = block_at(w, a, b)
        opposite = b == 2 or (b == 0 and a == 2)
        if opposite:
            for part in range(2):
                landed(weights.at[w, blk, pl.ds(part * 4, 4)], wxy_recv.at[w, blk, part])
        else:
            landed(weights.at[w, blk], wxy_recv.at[w, blk, 0])

    def forward(w, a, b, phase):
        if phase == 0:
            wxy(w, a, b, 0 if a == 1 else 1, 0, -1 if a == 1 else 1)
        else:
            wxy(w, a, b, 0 if b == 1 else 1, 1, -1 if b == 1 else 1)

    def plane0():
        for w in range(2):
            for phase in range(2):
                for sign in (1, -1):
                    wxy(w, 0, 0, None, phase, sign)

    def plane1():
        for w in range(2):
            for a in (1, 3):
                wxy_wait(w, a, 0)
                forward(w, a, 0, 0)
        for w in range(2):
            for b in (1, 3):
                wxy_wait(w, 0, b)
                forward(w, 0, b, 1)
        for w in range(2):
            for a in (1, 3):
                for sign in (1, -1):
                    wxy(w, a, 0, None, 1, sign)

    def plane2():
        for w in range(2):
            wxy_wait(w, 2, 0)
            for sign in (1, -1):
                wxy(w, 2, 0, None, 1, sign)
        for w in range(2):
            for a in (1, 3):
                for b in (1, 3):
                    wxy_wait(w, a, b)
                    forward(w, a, b, 1)

    def plane3():
        for w in range(2):
            for b in (1, 3):
                wxy_wait(w, 2, b)
                forward(w, 2, b, 1)

    def plane4(w):
        for a in range(4):
            wxy_wait(w, a, 2)

    ring_hop(0)
    ring_hop(1)
    wz_wait(5)
    wz_wait(6)
    plane0()
    loads[2].wait()
    loads[3].wait()
    expert(z, 0, z, 1)
    for slot in range(5):
        ring_wait(slot)
        ring_hop(slot + 2)
        expert_slot(slot)
        if slot == 2:
            plane1()

    def back_add(way, step):
        order, far, sign = ((BACK_DOWN, FAR_DOWN, 1), (BACK_UP, FAR_UP, -1))[way]
        half, k = order[step]
        if k < far[half]:
            slot = back_slot(far, half, k)
            landed(sums.at[way, slot], back_recv.at[way, slot])
            block = zmod(z - sign * k)
            partial[block, half] = (
                partial[block, half].astype(F32) + sums[way, slot].astype(F32)
            ).astype(BF16)

    def back_send_step(way, step):
        order, far, sign = ((BACK_DOWN, FAR_DOWN, 1), (BACK_UP, FAR_UP, -1))[way]
        half, k = order[step]
        slot = back_slot(far, half, k - 1)
        send(
            partial.at[zmod(z - sign * k), half], sums.at[way, slot], back_send.at[way, step],
            back_recv.at[way, slot], (z_down, z_up)[way],
        )

    ring_wait(5)
    expert_slot(5)
    for way in range(2):
        back_send_step(way, 0)
    ring_wait(6)
    expert_slot(6)
    for step in range(1, 7):
        for way in range(2):
            back_add(way, step)
            back_send_step(way, step)
        if step == 1:
            plane2()
        if step == 4:
            plane3()

    q_iota = lax.broadcasted_iota(jnp.int32, (E * 8, HALF), 0)
    r_iota = lax.broadcasted_iota(jnp.int32, (E * 8, HALF), 1)
    c_iota = q_iota % 8
    source = jnp.where(c_iota < C, (q_iota // 16) * C + c_iota, -1)
    low = (q_iota // 8) % 2 == 0
    unfold0 = ((r_iota == source) & low).astype(F32).astype(BF16)
    unfold1 = ((r_iota == source) & jnp.logical_not(low)).astype(F32).astype(BF16)
    for half in range(2):
        slot_d, slot_u = back_slot(FAR_DOWN, half, 0), back_slot(FAR_UP, half, 0)
        landed(sums.at[0, slot_d], back_recv.at[0, slot_d])
        landed(sums.at[1, slot_u], back_recv.at[1, slot_u])
        total[...] = (
            partial[z, half].astype(F32) + sums[0, slot_d].astype(F32) + sums[1, slot_u].astype(F32)
        ).astype(BF16)
        got = jnp.dot(unfold0, total[:, :hw], preferred_element_type=F32) + jnp.dot(
            unfold1, total[:, hw:], preferred_element_type=F32
        )
        returning[half * (E // 2):(half + 1) * (E // 2)] = got.astype(BF16).reshape(E // 2, 16, hw)

    for i, (yy, xx) in enumerate(peers):
        peer = yy * NX + xx
        send(returning.at[peer], returned.at[e], ret_send.at[i], ret_recv.at[e], peer * NZ + z)
    own_back = pltpu.make_async_copy(returning.at[e], returned.at[e], load_sem.at[5])
    own_back.start()
    plane4(0)
    plane4(1)
    place = place_ref[...]
    token_iota = lax.broadcasted_iota(jnp.int32, (rows, E * 16), 1)
    put0 = (token_iota == place).astype(F32).astype(BF16)
    put1 = (token_iota == place + 8).astype(F32).astype(BF16)
    own_back.wait()
    for yy, xx in peers:
        peer = yy * NX + xx
        landed(returned.at[peer], ret_recv.at[peer])
    gate = gate_ref[...]
    for half, put in enumerate((put0, put1)):
        for j in range(hw // 256):
            c = j * 256
            got = jnp.dot(put, returned[:, :, c:c + 256].reshape(E * 16, 256), preferred_element_type=F32)
            cols = slice(half * hw + c, half * hw + c + 256)
            mixed[:, cols] = hid[:, cols].astype(F32) + got * gate

    def norm_out(i, carry):
        at_rows = pl.ds(pl.multiple_of(i * 32, 32), 32)
        normed[at_rows, :] = norm_rows(mixed[at_rows, :], final_gain[...]).astype(BF16)
        return carry

    lax.fori_loop(0, rows // 32, norm_out, 0)

    def weight_cols(w, cols):
        return weights[w, :, :, :, cols].reshape(width, 256)

    def kv_copy(w):
        return pltpu.make_async_remote_copy(
            src_ref=kv_out.at[w], dst_ref=kv_in.at[w], send_sem=kv_send.at[w], recv_sem=kv_recv.at[w],
            device_id={"grp": 1 - grp}, device_id_type=pl.DeviceIdType.MESH,
        )

    @pl.when(grp == 0)
    def _():
        for w in range(2):
            def project(j, carry):
                cols = pl.ds(pl.multiple_of(j * 256, 256), 256)
                kv_out[w, :, cols] = jnp.dot(
                    normed[...], weight_cols(w, cols), preferred_element_type=F32
                ).astype(BF16)
                return carry

            lax.fori_loop(0, hw // 256, project, 0)
            kv_copy(w).start()
        out_ref[...] = normed[...]
        for w in range(2):
            kv_copy(w).wait_send()

    @pl.when(grp == 1)
    def _():
        def project(j, carry):
            cols = pl.ds(pl.multiple_of(j * 256, 256), 256)
            query[:, cols] = jnp.dot(
                normed[:ROWS_Q, :], weight_cols(0, cols), preferred_element_type=F32
            ).astype(BF16)
            return carry

        lax.fori_loop(0, hw // 256, project, 0)
        out_ref[ROWS_Q:, :] = mixed[ROWS_Q:, :].astype(BF16)

        q_pos = lax.broadcasted_iota(jnp.int32, (ROWS_Q, 1), 0)
        k_pos = lax.broadcasted_iota(jnp.int32, (1, rows), 1)
        seg_q = jnp.zeros((ROWS_Q, 1), jnp.int32)
        seg_k = jnp.zeros((1, rows), jnp.int32)
        q_end = jnp.zeros((1, 1), jnp.int32)
        k_end = jnp.zeros((1, 1), jnp.int32)
        for i in range(SENT):
            q_end = q_end + tgt_ref[:, i:i + 1]
            k_end = k_end + src_ref[:, i:i + 1]
            seg_q = seg_q + jnp.where(q_pos >= q_end, 1, 0)
            seg_k = seg_k + jnp.where(k_pos >= k_end, 1, 0)
        valid = seg_q < SENT
        allowed = (seg_q == seg_k) & valid
        for w in range(2):
            kv_copy(w).wait_recv()
        for h in range(hw // HD):
            cols = slice(h * HD, (h + 1) * HD)
            scores = lax.dot_general(
                query[:, cols], kv_in[0, :, cols], (((1,), (1,)), ((), ())), preferred_element_type=F32
            ) * HD ** (-0.5)
            scores = jnp.where(allowed, scores, -1e30)
            top = jnp.max(scores, axis=-1, keepdims=True)
            expd = jnp.exp(scores - top)
            prob = (expd / jnp.sum(expd, axis=-1, keepdims=True)).astype(BF16)
            context[:, cols] = jnp.dot(prob, kv_in[1, :, cols], preferred_element_type=F32).astype(BF16)
        for j in range(width // 256):
            cols = slice(j * 256, (j + 1) * 256)
            wo_rows = weights[1, j * 2:(j + 1) * 2].reshape(256, hw)
            attended = lax.dot_general(
                context[...], wo_rows, (((1,), (1,)), ((), ())), preferred_element_type=F32
            )
            attended = jnp.where(valid, attended, 0.0)
            out_ref[:ROWS_Q, cols] = (mixed[:ROWS_Q, cols] + attended).astype(BF16)

    for copy in sent:
        copy.wait_send()


def body(
    hidden, norm_gain, final_gain, router, w_in, w_out, expert_ids, slot_ids, src_len, tgt_len, wq, wk, wv, wo,
):
    rows, width = hidden.shape[1:]
    hw = wq.shape[1]
    ff = w_in.shape[2]
    vmem = pl.BlockSpec(memory_space=pltpu.VMEM)
    anywhere = pl.BlockSpec(memory_space=pl.ANY)
    dma = pltpu.SemaphoreType.DMA
    out = pl.pallas_call(
        kernel,
        out_shape=jax.ShapeDtypeStruct((rows, width), BF16),
        in_specs=[anywhere, vmem, vmem, anywhere, anywhere, anywhere] + [vmem] * 8,
        out_specs=vmem,
        scratch_shapes=[
            pltpu.VMEM((rows, width), BF16),
            pltpu.VMEM((rows, width), BF16),
            pltpu.VMEM((width, 128), BF16),
            pltpu.VMEM((width, ff), BF16),
            pltpu.VMEM((ff, width), BF16),
            pltpu.VMEM((E, 16, hw), BF16),
            pltpu.VMEM((E, 16, hw), BF16),
            pltpu.VMEM((NZ, 2, HALF, width), BF16),
            pltpu.VMEM((NZ, 2, HALF, width), BF16),
            pltpu.VMEM((2, 7, HALF, width), BF16),
            pltpu.VMEM((2 * HALF, ff), BF16),
            pltpu.VMEM((HALF, width), BF16),
            pltpu.VMEM((E, 16, hw), BF16),
            pltpu.VMEM((E, 16, hw), BF16),
            pltpu.VMEM((rows, width), F32),
            pltpu.VMEM((2, E, NZ, 16, hw), BF16),
            pltpu.VMEM((2, rows, hw), BF16),
            pltpu.VMEM((2, rows, hw), BF16),
            pltpu.VMEM((ROWS_Q, hw), BF16),
            pltpu.VMEM((ROWS_Q, hw), BF16),
            pltpu.VMEM((rows, 1), F32),
            pltpu.VMEM((rows, 1), jnp.int32),
            dma((6,)),
            dma((15,)),
            dma((E,)),
            dma((2, 7)),
            dma((2, 7)),
            dma((2, 7)),
            dma((2, 7)),
            dma((2, 7)),
            dma((2, 7)),
            dma((48,)),
            dma((2, E, 2)),
            dma((15,)),
            dma((E,)),
            dma((2,)),
            dma((2,)),
        ],
        compiler_params=pltpu.CompilerParams(
            collective_id=0, has_side_effects=True, vmem_limit_bytes=56 * 1024 * 1024
        ),
        cost_estimate=pl.CostEstimate(flops=10**10, bytes_accessed=12 * 10**6, transcendentals=10**6),
    )(
        hidden[0], norm_gain, final_gain, router[0], w_in[0], w_out[0], expert_ids[0].T, slot_ids[0].T,
        src_len, tgt_len, wq, wk, wv, wo,
    )
    return out[None]


def solution(mesh):
    in_specs = (
        P("grp", "ep", None),
        P("grp", None),
        P("grp", None),
        P("grp", None, None),
        P("grp", None, "ep"),
        P("grp", "ep", None),
        P("grp", "ep", None),
        P("grp", "ep", None),
        P("ep", None),
        P("ep", None),
        P("ep", None),
        P("ep", None),
        P("ep", None),
        P("ep", None),
    )
    out_specs = P("grp", "ep", None)
    return jax.shard_map(body, mesh=mesh, in_specs=in_specs, out_specs=out_specs, check_vma=False)
```

```python
import jax
import jax.numpy as jnp
from jax import lax
from jax.experimental import pallas as pl
from jax.experimental.pallas import tpu as pltpu
from jax.sharding import PartitionSpec as P

NY, NX, NZ = 4, 4, 8
E = NY * NX
C = 6
TRIO = C // 2
HALF = E * TRIO
SENT = 4
HD = 128
ROWS_Q = 176
F32 = jnp.float32
BF16 = jnp.bfloat16

RING = [(0, 1), (1, 1), (0, 2), (1, 2), (0, 3), (1, 3), (0, 4), (1, 4)]
BACK = [
    (0, 3, "near"), (1, 3, "near"), (0, 4, "far"), (1, 4, "far"), (0, 3, "far"), (1, 3, "far"),
    (0, 2, "all"), (1, 2, "all"), (0, 1, "all"), (1, 1, "all"),
]


def norm_rows(v, gain):
    mean = jnp.mean(v, -1, keepdims=True)
    centred = v - mean
    spread = jnp.mean(centred * centred, -1, keepdims=True)
    return centred * lax.rsqrt(spread + 1e-05) * gain


def one_hot(hit):
    return hit.astype(F32).astype(BF16)


def kernel(
    hidden_hbm, norm_gain, final_gain, router_hbm, w_in_hbm, w_out_hbm, ids_ref, slots_ref, src_ref, tgt_ref,
    wq_hbm, wk_hbm, wv_hbm, wo_hbm,
    out_ref,
    hid, normed, router, w_in, w_out, packed, arrived, tokens, partial, sums, inner, total, returning, returned,
    mixed, weights, kv_out, kv_in, query, context, gate_ref, pick, put, fold, unfold,
    load_sem, pack_send, pack_recv, ring_send, ring_recv, back_send, back_recv, wz_send, wz_recv,
    wxy_send, wxy_recv, ret_send, ret_recv, kv_send, kv_recv,
):
    rows, width = hid.shape
    hw = width // 2
    quarter = width // 4
    ep = lax.axis_index("ep")
    grp = lax.axis_index("grp")
    z = lax.rem(ep, NZ)
    e = ep // NZ
    x = lax.rem(e, NX)
    y = e // NX

    def at(yy, xx, zz):
        return (yy * NX + xx) * NZ + zz

    def zmod(v):
        return lax.rem(v + NZ, NZ)

    def xmod(v):
        return lax.rem(v + NX, NX)

    def remote(src, dst, send, recv, target):
        return pltpu.make_async_remote_copy(
            src_ref=src, dst_ref=dst, send_sem=send, recv_sem=recv,
            device_id={"ep": target}, device_id_type=pl.DeviceIdType.MESH,
        )

    sent = []

    def send(*args):
        copy = remote(*args)
        copy.start()
        sent.append(copy)

    def landed(dst, recv):
        remote(dst, dst, kv_send.at[0], recv, ep).wait_recv()

    z_up, z_down = at(y, x, zmod(z + 1)), at(y, x, zmod(z - 1))
    peers = []
    for dy in (2, 1, 3, 0):
        for dx in (2, 1, 3, 0):
            if dy or dx:
                peers.append((xmod(y + dy), xmod(x + dx)))

    load_hidden = pltpu.make_async_copy(hidden_hbm, hid, load_sem.at[0])
    load_router = pltpu.make_async_copy(router_hbm, router, load_sem.at[1])
    load_in = pltpu.make_async_copy(w_in_hbm, w_in, load_sem.at[2])
    load_out = pltpu.make_async_copy(w_out_hbm, w_out, load_sem.at[3])

    def load_rows(w, source):
        return pltpu.make_async_copy(source, weights.at[w, e, z], load_sem.at[4 + w])

    load_hidden.start()

    @pl.when(grp == 0)
    def _():
        load_rows(0, wk_hbm).start()
        load_rows(1, wv_hbm).start()

    @pl.when(grp == 1)
    def _():
        load_rows(0, wq_hbm).start()
        load_rows(1, wo_hbm).start()

    barrier = pltpu.get_barrier_semaphore()
    for target in [at(yy, xx, z) for yy, xx in peers] + [at(y, x, zmod(z + k)) for k in (-2, -1, 1, 2)]:
        pl.semaphore_signal(barrier, inc=1, device_id={"ep": target}, device_id_type=pl.DeviceIdType.MESH)
    pl.semaphore_signal(barrier, inc=1, device_id={"grp": 1 - grp}, device_id_type=pl.DeviceIdType.MESH)
    load_router.start()
    load_in.start()
    load_out.start()

    ids_row = ids_ref[...]
    slots_row = slots_ref[...]
    spots = []
    for half in range(2):
        live_row = (slots_row >= half * TRIO) & (slots_row < (half + 1) * TRIO)
        spot = jnp.where(live_row, ids_row * 16 + slots_row - half * TRIO, -1000)
        spots.append(jnp.max(spot, axis=0, keepdims=True))
    stacked = jnp.concatenate([ids_row, slots_row] + spots + spots, axis=0)
    columns = jnp.transpose(stacked.astype(F32)).astype(jnp.int32)
    ids, live = columns[:, 0:2], columns[:, 2:4] >= 0
    slot_iota = lax.broadcasted_iota(jnp.int32, (E * 16, rows), 0)
    for half in range(2):
        for q in range(4):
            pick[half, q] = one_hot(slot_iota == spots[half] + 4 * q)
    r_iota = lax.broadcasted_iota(jnp.int32, (HALF, E * 16), 0)
    q_iota = lax.broadcasted_iota(jnp.int32, (HALF, E * 16), 1)
    base = (r_iota // TRIO) * 16 + r_iota % TRIO
    for q in range(4):
        fold[q] = one_hot(q_iota == base + 4 * q)

    pl.semaphore_wait(barrier, len(peers) + 5)
    load_rows(0, wq_hbm).wait()
    load_rows(1, wq_hbm).wait()

    def ways():
        return enumerate(((1, z_up), (-1, z_down)))

    def part(ref, way, k):
        if k < 4:
            return ref
        size = ref.shape[-1] // 2
        return ref.at[:, pl.ds(way * size, size)]

    def wz_send_rows(w, block, way, reach, dist):
        ref = part(weights.at[w, e, block], way, dist)
        target = at(y, x, zmod(z + (reach, -reach)[way]))
        send(ref, ref, wz_send.at[w, way, dist - 1], wz_recv.at[w, way, dist - 1], target)

    def wz_wait(w, way, dist):
        block = zmod(z - (dist, -dist)[way])
        landed(part(weights.at[w, e, block], way, dist), wz_recv.at[w, way, dist - 1])

    def wz_near():
        for dist in (2, 1):
            for w in range(2):
                for way in range(2):
                    wz_send_rows(w, z, way, dist, dist)

    def wz_far():
        for w in range(2):
            for way in range(2):
                wz_wait(w, way, 2)
                block = zmod(z - (2, -2)[way])
                wz_send_rows(w, block, way, 1, 3)
                wz_send_rows(w, block, way, 2, 4)

    def wz_end():
        for w in range(2):
            for way in range(2):
                for dist in (1, 3, 4):
                    wz_wait(w, way, dist)

    wz_near()

    load_hidden.wait()

    def norm_in(i, carry):
        at_rows = pl.ds(pl.multiple_of(i * 32, 32), 32)
        normed[at_rows, :] = norm_rows(hid[at_rows, :].astype(F32), norm_gain[...]).astype(BF16)
        return carry

    lax.fori_loop(0, rows // 32, norm_in, 0)

    own_slots = [pltpu.make_async_copy(packed.at[h, e], arrived.at[h, e], load_sem.at[6 + h]) for h in range(2)]
    own_back = [
        pltpu.make_async_copy(returning.at[h, e], returned.at[h, e], load_sem.at[8 + h]) for h in range(2)
    ]
    for half in range(2):
        for j in range(quarter // 256):
            got = jnp.zeros((E * 16, 256), F32)
            for q in range(4):
                c = q * quarter + j * 256
                got = got + jnp.dot(pick[half, q], normed[:, c:c + 256], preferred_element_type=F32)
            packed[half, :, :, j * 256:(j + 1) * 256] = got.astype(BF16).reshape(E, 16, 256)
        for i, (yy, xx) in enumerate(peers):
            peer = yy * NX + xx
            send(
                packed.at[half, peer], arrived.at[half, e], pack_send.at[half, i], pack_recv.at[half, e],
                peer * NZ + z,
            )
        own_slots[half].start()

    def slots_in(half):
        own_slots[half].wait()
        for yy, xx in peers:
            peer = yy * NX + xx
            landed(arrived.at[half, peer], pack_recv.at[half, peer])
        got = arrived[half].reshape(E * 16, quarter)
        for q in range(4):
            tokens[z, half, :, q * quarter:(q + 1) * quarter] = jnp.dot(
                fold[q], got, preferred_element_type=F32
            ).astype(BF16)

    def ring_hop(slot):
        half, k = RING[slot]
        for way, (sign, target) in ways():
            ref = part(tokens.at[zmod(z - sign * (k - 1)), half], way, k)
            send(ref, ref, ring_send.at[way, slot], ring_recv.at[way, slot], target)

    def ring_wait(slot):
        half, k = RING[slot]
        for way, (sign, _) in ways():
            landed(part(tokens.at[zmod(z - sign * k), half], way, k), ring_recv.at[way, slot])

    def expert(parts):
        count = len(parts) * HALF

        def first_step(j, carry):
            cols = pl.ds(pl.multiple_of(j * 256, 256), 256)
            blocks = [tokens[block, half] for block, half in parts]
            both = jnp.concatenate(blocks, axis=0) if len(blocks) > 1 else blocks[0]
            got = jnp.dot(both, w_in[:, cols], preferred_element_type=F32)
            inner[:count, cols] = jnp.maximum(got, 0.0).astype(BF16)
            return carry

        def second_step(j, carry):
            cols = pl.ds(pl.multiple_of(j * 256, 256), 256)
            got = jnp.dot(inner[:count, :], w_out[:, cols], preferred_element_type=F32).astype(BF16)
            for i, (block, half) in enumerate(parts):
                partial[block, half, :, cols] = got[i * HALF:(i + 1) * HALF]
            return carry

        lax.fori_loop(0, w_in.shape[1] // 256, first_step, 0)
        lax.fori_loop(0, width // 256, second_step, 0)

    def expert_slot(slot):
        half, k = RING[slot]
        expert([(zmod(z - k), half), (zmod(z + k), half)] if k < 4 else [(zmod(z + k), half)])

    def block_at(w, a, b):
        xx, yy = (xmod(x + a), xmod(y + b)) if w == 0 else (xmod(x + b), xmod(y + a))
        return yy * NX + xx

    def go(w, phase, sign):
        if (w == 0) == (phase == 0):
            return at(y, xmod(x + sign), z)
        return at(xmod(y + sign), x, z)

    w_count = [0]

    def wxy(w, a, b, piece, phase, sign):
        blk = block_at(w, a, b)
        ref = weights.at[w, blk] if piece is None else weights.at[w, blk, pl.ds(piece * 4, 4)]
        send(ref, ref, wxy_send.at[w_count[0]], wxy_recv.at[w, blk, piece or 0], go(w, phase, sign))
        w_count[0] += 1

    def wxy_wait(w, a, b):
        blk = block_at(w, a, b)
        opposite = b == 2 or (b == 0 and a == 2)
        if opposite:
            for piece in range(2):
                landed(weights.at[w, blk, pl.ds(piece * 4, 4)], wxy_recv.at[w, blk, piece])
        else:
            landed(weights.at[w, blk], wxy_recv.at[w, blk, 0])

    def forward(w, a, b, phase):
        if phase == 0:
            wxy(w, a, b, 0 if a == 1 else 1, 0, -1 if a == 1 else 1)
        else:
            wxy(w, a, b, 0 if b == 1 else 1, 1, -1 if b == 1 else 1)

    def plane0():
        for w in range(2):
            for phase in range(2):
                for sign in (1, -1):
                    wxy(w, 0, 0, None, phase, sign)

    def plane1():
        for w in range(2):
            for a in (1, 3):
                wxy_wait(w, a, 0)
                forward(w, a, 0, 0)
        for w in range(2):
            for b in (1, 3):
                wxy_wait(w, 0, b)
                forward(w, 0, b, 1)
        for w in range(2):
            for a in (1, 3):
                for sign in (1, -1):
                    wxy(w, a, 0, None, 1, sign)

    def plane2():
        for w in range(2):
            wxy_wait(w, 2, 0)
            for sign in (1, -1):
                wxy(w, 2, 0, None, 1, sign)
        for w in range(2):
            for a in (1, 3):
                for b in (1, 3):
                    wxy_wait(w, a, b)
                    forward(w, a, b, 1)

    def plane3():
        for w in range(2):
            for b in (1, 3):
                wxy_wait(w, 2, b)
                forward(w, 2, b, 1)

    def plane4(w):
        for a in range(4):
            wxy_wait(w, a, 2)

    wz_far()
    def columns_of(ref, way, kind):
        if kind == "all":
            return ref
        size = ref.shape[-1] // 2
        return ref.at[:, pl.ds((way if kind == "far" else 1 - way) * size, size)]

    def back_step(step):
        half, k, kind = BACK[step]
        for way, (sign, target) in enumerate(((1, z_down), (-1, z_up))):
            here = columns_of(partial.at[zmod(z - sign * k), half], way, kind)
            came = columns_of(sums.at[way, half, min(k, 3)], way, kind)
            if k == 2:
                for i, other in enumerate(("far", "near")):
                    landed(columns_of(sums.at[way, half, 2], way, other), back_recv.at[way, half, 2, i])
            elif k == 1 or (k == 3 and kind == "far"):
                landed(came, back_recv.at[way, half, k, 0])
            if k < 3 or (k == 3 and kind == "far"):
                here[...] = (here[...].astype(F32) + came[...].astype(F32)).astype(BF16)
            send(
                here, columns_of(sums.at[way, half, k - 1], way, kind), back_send.at[way, step],
                back_recv.at[way, half, k - 1, 1 if kind == "near" else 0], target,
            )

    slots_in(0)
    ring_hop(0)
    slots_in(1)
    ring_hop(1)
    load_in.wait()
    load_out.wait()
    wz_end()
    plane0()
    expert([(z, 0), (z, 1)])
    for slot in range(6):
        ring_wait(slot)
        ring_hop(slot + 2)
        if slot == 5:
            back_step(0)
        expert_slot(slot)
        if slot == 0:
            load_router.wait()
            logits = jnp.dot(normed[...], router[...], preferred_element_type=F32)
            lane = lax.broadcasted_iota(jnp.int32, logits.shape, 1)
            pick_a = jnp.sum(jnp.where(lane == ids[:, 0:1], logits, 0.0), axis=1, keepdims=True)
            pick_b = jnp.sum(jnp.where(lane == ids[:, 1:2], logits, 0.0), axis=1, keepdims=True)
            gate_ref[...] = jnp.where(live[:, 0:1], jax.nn.sigmoid(pick_a - pick_b), 0.0) + jnp.where(
                live[:, 1:2], jax.nn.sigmoid(pick_b - pick_a), 0.0
            )
        if slot == 1:
            token_iota = lax.broadcasted_iota(jnp.int32, (rows, E * 16), 1)
            for half in range(2):
                for q in range(4):
                    put[half, q] = one_hot(token_iota == columns[:, 4 + half:5 + half] + 4 * q)
        if slot == 2:
            b_iota = lax.broadcasted_iota(jnp.int32, (E * 16, HALF), 0)
            s_iota = lax.broadcasted_iota(jnp.int32, (E * 16, HALF), 1)
            origin = (s_iota // TRIO) * 16 + s_iota % TRIO
            for q in range(4):
                unfold[q] = one_hot(b_iota == origin + 4 * q)
        if slot == 3:
            plane1()

    back_step(1)
    ring_wait(6)
    ring_wait(7)
    expert([(zmod(z + 4), 0), (zmod(z + 4), 1)])
    back_step(2)
    back_step(3)
    plane2()
    for step in range(4, len(BACK)):
        back_step(step)
        if step == 6:
            plane3()

    for half in range(2):
        for way in range(2):
            landed(sums.at[way, half, 0], back_recv.at[way, half, 0, 0])
        total[...] = (
            partial[z, half].astype(F32) + sums[0, half, 0].astype(F32) + sums[1, half, 0].astype(F32)
        ).astype(BF16)
        got = jnp.zeros((E * 16, quarter), F32)
        for q in range(4):
            got = got + jnp.dot(
                unfold[q], total[:, q * quarter:(q + 1) * quarter], preferred_element_type=F32
            )
        returning[half] = got.astype(BF16).reshape(E, 16, quarter)
        for i, (yy, xx) in enumerate(peers):
            peer = yy * NX + xx
            send(
                returning.at[half, peer], returned.at[half, e], ret_send.at[half, i], ret_recv.at[half, e],
                peer * NZ + z,
            )
        own_back[half].start()
    plane4(0)
    for half in range(2):
        own_back[half].wait()
        for yy, xx in peers:
            peer = yy * NX + xx
            landed(returned.at[half, peer], ret_recv.at[half, peer])
        gate = gate_ref[...]
        for q in range(4):
            for j in range(quarter // 256):
                got = jnp.dot(
                    put[half, q], returned[half, :, :, j * 256:(j + 1) * 256].reshape(E * 16, 256),
                    preferred_element_type=F32,
                )
                c = q * quarter + j * 256
                before = mixed[:, c:c + 256] if half else hid[:, c:c + 256].astype(F32)
                mixed[:, c:c + 256] = before + got * gate

    def norm_out(i, carry):
        at_rows = pl.ds(pl.multiple_of(i * 32, 32), 32)
        normed[at_rows, :] = norm_rows(mixed[at_rows, :], final_gain[...]).astype(BF16)
        return carry

    lax.fori_loop(0, rows // 32, norm_out, 0)
    plane4(1)

    groups = hw // 256

    def weight_cols(w, j):
        return weights[w, :, :, :, j * 256:(j + 1) * 256].reshape(width, 256)

    def kv_copy(j):
        return pltpu.make_async_remote_copy(
            src_ref=kv_out.at[j], dst_ref=kv_in.at[j], send_sem=kv_send.at[j], recv_sem=kv_recv.at[j],
            device_id={"grp": 1 - grp}, device_id_type=pl.DeviceIdType.MESH,
        )

    @pl.when(grp == 0)
    def _():
        for j in range(groups):
            for w in range(2):
                kv_out[j, w] = jnp.dot(
                    normed[...], weight_cols(w, j), preferred_element_type=F32
                ).astype(BF16)
            kv_copy(j).start()
        out_ref[...] = normed[...]
        for j in range(groups):
            kv_copy(j).wait_send()

    @pl.when(grp == 1)
    def _():
        for j in range(groups):
            query[j] = jnp.dot(
                normed[:ROWS_Q, :], weight_cols(0, j), preferred_element_type=F32
            ).astype(BF16)
        out_ref[ROWS_Q:, :] = mixed[ROWS_Q:, :].astype(BF16)

        q_pos = lax.broadcasted_iota(jnp.int32, (ROWS_Q, 1), 0)
        k_pos = lax.broadcasted_iota(jnp.int32, (1, rows), 1)
        seg_q = jnp.zeros((ROWS_Q, 1), jnp.int32)
        seg_k = jnp.zeros((1, rows), jnp.int32)
        q_end = jnp.zeros((1, 1), jnp.int32)
        k_end = jnp.zeros((1, 1), jnp.int32)
        for i in range(SENT):
            q_end = q_end + tgt_ref[:, i:i + 1]
            k_end = k_end + src_ref[:, i:i + 1]
            seg_q = seg_q + jnp.where(q_pos >= q_end, 1, 0)
            seg_k = seg_k + jnp.where(k_pos >= k_end, 1, 0)
        valid = seg_q < SENT
        allowed = (seg_q == seg_k) & valid
        for h in range(hw // HD):
            j, cols = h // 2, slice(h % 2 * HD, (h % 2 + 1) * HD)
            if h % 2 == 0:
                kv_copy(j).wait_recv()
            scores = lax.dot_general(
                query[j, :, cols], kv_in[j, 0, :, cols], (((1,), (1,)), ((), ())), preferred_element_type=F32
            ) * HD ** (-0.5)
            scores = jnp.where(allowed, scores, -1e30)
            top = jnp.max(scores, axis=-1, keepdims=True)
            expd = jnp.exp(scores - top)
            prob = (expd / jnp.sum(expd, axis=-1, keepdims=True)).astype(BF16)
            context[:, h * HD:(h + 1) * HD] = jnp.dot(
                prob, kv_in[j, 1, :, cols], preferred_element_type=F32
            ).astype(BF16)
        for j in range(width // 256):
            cols = slice(j * 256, (j + 1) * 256)
            wo_rows = weights[1, j * 2:(j + 1) * 2].reshape(256, hw)
            attended = lax.dot_general(
                context[...], wo_rows, (((1,), (1,)), ((), ())), preferred_element_type=F32
            )
            attended = jnp.where(valid, attended, 0.0)
            out_ref[:ROWS_Q, cols] = (mixed[:ROWS_Q, cols] + attended).astype(BF16)

    for copy in sent:
        copy.wait_send()


def body(
    hidden, norm_gain, final_gain, router, w_in, w_out, expert_ids, slot_ids, src_len, tgt_len, wq, wk, wv, wo,
):
    rows, width = hidden.shape[1:]
    hw = wq.shape[1]
    ff = w_in.shape[2]
    vmem = pl.BlockSpec(memory_space=pltpu.VMEM)
    anywhere = pl.BlockSpec(memory_space=pl.ANY)
    dma = pltpu.SemaphoreType.DMA
    out = pl.pallas_call(
        kernel,
        out_shape=pltpu.VMEM((rows, width), BF16),
        in_specs=[anywhere, vmem, vmem, anywhere, anywhere, anywhere] + [vmem] * 4 + [anywhere] * 4,
        out_specs=vmem,
        scratch_shapes=[
            pltpu.VMEM((rows, width), BF16),
            pltpu.VMEM((rows, width), BF16),
            pltpu.VMEM((width, 128), BF16),
            pltpu.VMEM((width, ff), BF16),
            pltpu.VMEM((ff, width), BF16),
            pltpu.VMEM((2, E, 16, width // 4), BF16),
            pltpu.VMEM((2, E, 16, width // 4), BF16),
            pltpu.VMEM((NZ, 2, HALF, width), BF16),
            pltpu.VMEM((NZ, 2, HALF, width), BF16),
            pltpu.VMEM((2, 2, 4, HALF, width), BF16),
            pltpu.VMEM((2 * HALF, ff), BF16),
            pltpu.VMEM((HALF, width), BF16),
            pltpu.VMEM((2, E, 16, width // 4), BF16),
            pltpu.VMEM((2, E, 16, width // 4), BF16),
            pltpu.VMEM((rows, width), F32),
            pltpu.VMEM((2, E, NZ, 16, hw), BF16),
            pltpu.VMEM((hw // 256, 2, rows, 256), BF16),
            pltpu.VMEM((hw // 256, 2, rows, 256), BF16),
            pltpu.VMEM((hw // 256, ROWS_Q, 256), BF16),
            pltpu.VMEM((ROWS_Q, hw), BF16),
            pltpu.VMEM((rows, 1), F32),
            pltpu.VMEM((2, 4, E * 16, rows), BF16),
            pltpu.VMEM((2, 4, rows, E * 16), BF16),
            pltpu.VMEM((4, HALF, E * 16), BF16),
            pltpu.VMEM((4, E * 16, HALF), BF16),
            dma((10,)),
            dma((2, 15)),
            dma((2, E)),
            dma((2, 8)),
            dma((2, 8)),
            dma((2, len(BACK))),
            dma((2, 2, 4, 2)),
            dma((2, 2, 4)),
            dma((2, 2, 4)),
            dma((40,)),
            dma((2, E, 2)),
            dma((2, 15)),
            dma((2, E)),
            dma((hw // 256,)),
            dma((hw // 256,)),
        ],
        compiler_params=pltpu.CompilerParams(
            collective_id=0, has_side_effects=True, vmem_limit_bytes=56 * 1024 * 1024
        ),
        cost_estimate=pl.CostEstimate(flops=10**10, bytes_accessed=12 * 10**6, transcendentals=10**6),
    )(
        hidden[0], norm_gain, final_gain, router[0], w_in[0], w_out[0], expert_ids[0].T, slot_ids[0].T,
        src_len, tgt_len, wq, wk, wv, wo,
    )
    return out[None]


def solution(mesh):
    in_specs = (
        P("grp", "ep", None),
        P("grp", None),
        P("grp", None),
        P("grp", None, None),
        P("grp", None, "ep"),
        P("grp", "ep", None),
        P("grp", "ep", None),
        P("grp", "ep", None),
        P("ep", None),
        P("ep", None),
        P("ep", None),
        P("ep", None),
        P("ep", None),
        P("ep", None),
    )
    out_specs = P("grp", "ep", None)
    return jax.shard_map(body, mesh=mesh, in_specs=in_specs, out_specs=out_specs, check_vma=False)
```

```python
import jax
import jax.numpy as jnp
from jax import lax
from jax.experimental import pallas as pl
from jax.experimental.pallas import tpu as pltpu
from jax.sharding import PartitionSpec as P

NY, NX, NZ = 4, 4, 8
E = NY * NX
C = 6
PAIR = 2 * E
START = (0, PAIR)
SIZE = (PAIR, 2 * PAIR)
PAIRS = ((0,), (1, 2))
SENT = 4
HD = 128
ROWS_Q = 176
F32 = jnp.float32
BF16 = jnp.bfloat16

RING = [(0, 1), (1, 1), (0, 2), (1, 2), (0, 3), (1, 3), (0, 4), (1, 4)]
BACK = [
    (0, 3, "near"), (1, 3, "near"), (1, 4, "far"), (0, 4, "far"), (1, 3, "far"), (0, 3, "far"),
    (1, 2, "all"), (0, 2, "all"), (1, 1, "all"), (0, 1, "all"),
]


def norm_rows(v, gain):
    mean = jnp.mean(v, -1, keepdims=True)
    centred = v - mean
    spread = jnp.mean(centred * centred, -1, keepdims=True)
    return centred * lax.rsqrt(spread + 1e-05) * gain


def one_hot(hit):
    return hit.astype(F32).astype(BF16)


def kernel(
    hidden_hbm, norm_gain, final_gain, router_hbm, w_in_hbm, w_out_hbm, ids_ref, slots_ref, src_ref, tgt_ref,
    wq_hbm, wk_hbm, wv_hbm, wo_hbm,
    out_ref,
    hid, normed, router, w_in, w_out, packed, arrived, tokens, partial, sums, inner, returning, returned,
    mixed, weights, kv_out, kv_in, query, context, gate_ref, spot_ref, pick, perm, perm_t, back_rows,
    load_sem, pack_send, pack_recv, ring_send, ring_recv, back_send, back_recv, wz_send, wz_recv,
    wxy_send, wxy_recv, ret_send, ret_recv, kv_send, kv_recv,
):
    rows, width = hid.shape
    hw = width // 2
    eighth = width // 8
    ep = lax.axis_index("ep")
    grp = lax.axis_index("grp")
    z = lax.rem(ep, NZ)
    e = ep // NZ
    x = lax.rem(e, NX)
    y = e // NX

    def at(yy, xx, zz):
        return (yy * NX + xx) * NZ + zz

    def zmod(v):
        return lax.rem(v + NZ, NZ)

    def xmod(v):
        return lax.rem(v + NX, NX)

    def remote(src, dst, send, recv, target):
        return pltpu.make_async_remote_copy(
            src_ref=src, dst_ref=dst, send_sem=send, recv_sem=recv,
            device_id={"ep": target}, device_id_type=pl.DeviceIdType.MESH,
        )

    sent = []

    def send(*args):
        copy = remote(*args)
        copy.start()
        sent.append(copy)

    def landed(dst, recv):
        remote(dst, dst, kv_send.at[0], recv, ep).wait_recv()

    z_up, z_down = at(y, x, zmod(z + 1)), at(y, x, zmod(z - 1))
    peers = []
    for dy in (2, 1, 3, 0):
        for dx in (2, 1, 3, 0):
            if dy or dx:
                peers.append((xmod(y + dy), xmod(x + dx)))

    load_hidden = pltpu.make_async_copy(hidden_hbm, hid, load_sem.at[0])
    load_router = pltpu.make_async_copy(router_hbm, router, load_sem.at[1])
    load_in = pltpu.make_async_copy(w_in_hbm, w_in, load_sem.at[2])
    load_out = pltpu.make_async_copy(w_out_hbm, w_out, load_sem.at[3])

    def load_rows(w, source):
        return pltpu.make_async_copy(source, weights.at[w, e, z], load_sem.at[4 + w])

    load_hidden.start()

    @pl.when(grp == 0)
    def _():
        load_rows(0, wk_hbm).start()
        load_rows(1, wv_hbm).start()

    @pl.when(grp == 1)
    def _():
        load_rows(0, wq_hbm).start()
        load_rows(1, wo_hbm).start()

    barrier = pltpu.get_barrier_semaphore()
    for target in [at(yy, xx, z) for yy, xx in peers] + [at(y, x, zmod(z + k)) for k in (-2, -1, 1, 2)]:
        pl.semaphore_signal(barrier, inc=1, device_id={"ep": target}, device_id_type=pl.DeviceIdType.MESH)
    pl.semaphore_signal(barrier, inc=1, device_id={"grp": 1 - grp}, device_id_type=pl.DeviceIdType.MESH)
    load_router.start()
    load_in.start()
    load_out.start()

    ids_row = ids_ref[...]
    slots_row = slots_ref[...]
    pair_row = jnp.where(slots_row >= 2, 1, 0) + jnp.where(slots_row >= 4, 1, 0)
    spot = jnp.where(slots_row >= 0, pair_row * (PAIR - 2) + 2 * ids_row + slots_row, -1000)
    spot = jnp.max(spot, axis=0, keepdims=True)
    stacked = jnp.concatenate([ids_row, slots_row] + [spot] * 4, axis=0)
    columns = jnp.transpose(stacked.astype(F32)).astype(jnp.int32)
    ids, live, spot_ref[...] = columns[:, 0:2], columns[:, 2:4] >= 0, columns[:, 4:5]
    pick[...] = one_hot(lax.broadcasted_iota(jnp.int32, (E * C, rows), 0) == spot)
    i_iota = lax.broadcasted_iota(jnp.int32, (E * 16, E * 16), 0)
    j_iota = lax.broadcasted_iota(jnp.int32, (E * 16, E * 16), 1)
    perm[...] = one_hot(j_iota == (i_iota % 16) // 2 * PAIR + i_iota // 16 * 2 + i_iota % 2)
    perm_t[...] = one_hot(i_iota == (j_iota % 16) // 2 * PAIR + j_iota // 16 * 2 + j_iota % 2)

    pl.semaphore_wait(barrier, len(peers) + 5)
    load_rows(0, wq_hbm).wait()
    load_rows(1, wq_hbm).wait()

    def ways():
        return enumerate(((1, z_up), (-1, z_down)))

    def part(ref, way, k):
        if k < 4:
            return ref
        size = ref.shape[-1] // 2
        return ref.at[:, pl.ds(way * size, size)]

    def wz_send_rows(w, block, way, reach, dist):
        ref = part(weights.at[w, e, block], way, dist)
        target = at(y, x, zmod(z + (reach, -reach)[way]))
        send(ref, ref, wz_send.at[w, way, dist - 1], wz_recv.at[w, way, dist - 1], target)

    def wz_wait(w, way, dist):
        block = zmod(z - (dist, -dist)[way])
        landed(part(weights.at[w, e, block], way, dist), wz_recv.at[w, way, dist - 1])

    def wz_near():
        for dist in (2, 1):
            for w in range(2):
                for way in range(2):
                    wz_send_rows(w, z, way, dist, dist)

    def wz_far():
        for w in range(2):
            for way in range(2):
                wz_wait(w, way, 2)
                block = zmod(z - (2, -2)[way])
                wz_send_rows(w, block, way, 1, 3)
                wz_send_rows(w, block, way, 2, 4)

    def wz_end():
        for w in range(2):
            for way in range(2):
                for dist in (1, 3, 4):
                    wz_wait(w, way, dist)

    wz_near()

    load_hidden.wait()

    def norm_in(i, carry):
        for j in range(4):
            at_rows = pl.ds(pl.multiple_of(i * 64 + j * 16, 16), 16)
            normed[at_rows, :] = norm_rows(hid[at_rows, :].astype(F32), norm_gain[...]).astype(BF16)
        return carry

    def spread(pair_rows):
        tall = jnp.concatenate([pair_rows[:, q * eighth:(q + 1) * eighth] for q in range(8)], axis=0)
        return jnp.dot(perm[...], tall, preferred_element_type=F32).astype(BF16).reshape(E, 16, eighth)

    def gathered(ref, pair):
        tall = jnp.dot(
            perm_t[...], ref[:, :, pair * eighth:(pair + 1) * eighth].reshape(E * 16, eighth),
            preferred_element_type=F32,
        )
        return jnp.concatenate([tall[q * PAIR:(q + 1) * PAIR] for q in range(8)], axis=1)

    def piece(ref, block, half):
        return ref.at[block, pl.ds(START[half], SIZE[half])]

    def exchange(source, target, send_sem, recv_sem, half):
        for i, (yy, xx) in enumerate(peers):
            peer = yy * NX + xx
            send(
                pair_cols_at(source, peer, half), pair_cols_at(target, e, half), send_sem.at[half, i],
                recv_sem.at[half, e], peer * NZ + z,
            )

    def pair_cols_at(ref, block, half):
        return ref.at[block, :, pl.ds(PAIRS[half][0] * eighth, len(PAIRS[half]) * eighth)]

    def exchanged(target, recv_sem, half):
        for yy, xx in peers:
            peer = yy * NX + xx
            landed(pair_cols_at(target, peer, half), recv_sem.at[half, peer])

    own_slots = [
        pltpu.make_async_copy(pair_cols_at(packed, e, h), pair_cols_at(arrived, e, h), load_sem.at[6 + h])
        for h in range(2)
    ]
    own_back = [
        pltpu.make_async_copy(pair_cols_at(returning, e, h), pair_cols_at(returned, e, h), load_sem.at[8 + h])
        for h in range(2)
    ]
    for half in range(2):
        picked = jnp.dot(
            pick[START[half]:START[half] + SIZE[half], :], hid[...], preferred_element_type=F32
        ).astype(BF16)
        for i, pair in enumerate(PAIRS[half]):
            packed[:, :, pair * eighth:(pair + 1) * eighth] = spread(picked[i * PAIR:(i + 1) * PAIR])
        exchange(packed, arrived, pack_send, pack_recv, half)
        own_slots[half].start()

    def slots_in(half):
        own_slots[half].wait()
        exchanged(arrived, pack_recv, half)
        for pair in PAIRS[half]:
            tokens[z, pair * PAIR:(pair + 1) * PAIR, :] = norm_rows(
                gathered(arrived, pair), norm_gain[...]
            ).astype(BF16)

    def ring_hop(slot):
        half, k = RING[slot]
        for way, (sign, target) in ways():
            ref = part(piece(tokens, zmod(z - sign * (k - 1)), half), way, k)
            send(ref, ref, ring_send.at[way, slot], ring_recv.at[way, slot], target)

    def ring_wait(slot):
        half, k = RING[slot]
        for way, (sign, _) in ways():
            landed(part(piece(tokens, zmod(z - sign * k), half), way, k), ring_recv.at[way, slot])

    def expert(parts):
        count = sum(SIZE[half] for _, half in parts)

        def first_step(j, carry):
            cols = pl.ds(pl.multiple_of(j * 256, 256), 256)
            blocks = [tokens[block, START[half]:START[half] + SIZE[half]] for block, half in parts]
            both = jnp.concatenate(blocks, axis=0)
            got = jnp.dot(both, w_in[:, cols], preferred_element_type=F32)
            inner[:count, cols] = jnp.maximum(got, 0.0).astype(BF16)
            return carry

        def second_step(j, carry):
            cols = pl.ds(pl.multiple_of(j * 256, 256), 256)
            got = jnp.dot(inner[:count, :], w_out[:, cols], preferred_element_type=F32).astype(BF16)
            row = 0
            for block, half in parts:
                partial[block, START[half]:START[half] + SIZE[half], cols] = got[row:row + SIZE[half]]
                row += SIZE[half]
            return carry

        lax.fori_loop(0, w_in.shape[1] // 256, first_step, 0)
        lax.fori_loop(0, width // 256, second_step, 0)

    def expert_slot(slot):
        half, k = RING[slot]
        expert([(zmod(z - k), half), (zmod(z + k), half)] if k < 4 else [(zmod(z + k), half)])

    def block_at(w, a, b):
        xx, yy = (xmod(x + a), xmod(y + b)) if w == 0 else (xmod(x + b), xmod(y + a))
        return yy * NX + xx

    def go(w, phase, sign):
        if (w == 0) == (phase == 0):
            return at(y, xmod(x + sign), z)
        return at(xmod(y + sign), x, z)

    w_count = [0]

    def wxy(w, a, b, piece, phase, sign):
        blk = block_at(w, a, b)
        ref = weights.at[w, blk] if piece is None else weights.at[w, blk, pl.ds(piece * 4, 4)]
        send(ref, ref, wxy_send.at[w_count[0]], wxy_recv.at[w, blk, piece or 0], go(w, phase, sign))
        w_count[0] += 1

    def wxy_wait(w, a, b):
        blk = block_at(w, a, b)
        opposite = b == 2 or (b == 0 and a == 2)
        if opposite:
            for piece in range(2):
                landed(weights.at[w, blk, pl.ds(piece * 4, 4)], wxy_recv.at[w, blk, piece])
        else:
            landed(weights.at[w, blk], wxy_recv.at[w, blk, 0])

    def forward(w, a, b, phase):
        if phase == 0:
            wxy(w, a, b, 0 if a == 1 else 1, 0, -1 if a == 1 else 1)
        else:
            wxy(w, a, b, 0 if b == 1 else 1, 1, -1 if b == 1 else 1)

    def plane0():
        for w in range(2):
            for phase in range(2):
                for sign in (1, -1):
                    wxy(w, 0, 0, None, phase, sign)

    def plane1():
        for w in range(2):
            for a in (1, 3):
                wxy_wait(w, a, 0)
                forward(w, a, 0, 0)
        for w in range(2):
            for b in (1, 3):
                wxy_wait(w, 0, b)
                forward(w, 0, b, 1)
        for w in range(2):
            for a in (1, 3):
                for sign in (1, -1):
                    wxy(w, a, 0, None, 1, sign)

    def plane2():
        for w in range(2):
            wxy_wait(w, 2, 0)
            for sign in (1, -1):
                wxy(w, 2, 0, None, 1, sign)
        for w in range(2):
            for a in (1, 3):
                for b in (1, 3):
                    wxy_wait(w, a, b)
                    forward(w, a, b, 1)

    def plane3():
        for w in range(2):
            for b in (1, 3):
                wxy_wait(w, 2, b)
                forward(w, 2, b, 1)

    def plane4(w):
        for a in range(4):
            wxy_wait(w, a, 2)

    wz_far()
    def columns_of(ref, way, kind):
        if kind == "all":
            return ref
        size = ref.shape[-1] // 2
        return ref.at[:, pl.ds((way if kind == "far" else 1 - way) * size, size)]

    def back_step(step):
        half, k, kind = BACK[step]
        for way, (sign, target) in enumerate(((1, z_down), (-1, z_up))):
            here = columns_of(piece(partial, zmod(z - sign * k), half), way, kind)
            came = columns_of(piece(sums.at[way], min(k, 3), half), way, kind)
            if k == 2:
                for i, other in enumerate(("far", "near")):
                    landed(columns_of(piece(sums.at[way], 2, half), way, other), back_recv.at[way, half, 2, i])
            elif k == 1 or (k == 3 and kind == "far"):
                landed(came, back_recv.at[way, half, k, 0])
            if k < 3 or (k == 3 and kind == "far"):
                here[...] = (here[...].astype(F32) + came[...].astype(F32)).astype(BF16)
            send(
                here, columns_of(piece(sums.at[way], k - 1, half), way, kind), back_send.at[way, step],
                back_recv.at[way, half, k - 1, 1 if kind == "near" else 0], target,
            )

    slots_in(0)
    ring_hop(0)
    slots_in(1)
    ring_hop(1)
    load_in.wait()
    load_out.wait()
    wz_end()
    plane0()
    expert([(z, 0), (z, 1)])
    for slot in range(6):
        ring_wait(slot)
        ring_hop(slot + 2)
        if slot == 5:
            back_step(0)
        expert_slot(slot)
        if slot == 1:
            load_router.wait()
            lax.fori_loop(0, rows // 64, norm_in, 0)
            logits = jnp.dot(normed[...], router[...], preferred_element_type=F32)
            lane = lax.broadcasted_iota(jnp.int32, logits.shape, 1)
            pick_a = jnp.sum(jnp.where(lane == ids[:, 0:1], logits, 0.0), axis=1, keepdims=True)
            pick_b = jnp.sum(jnp.where(lane == ids[:, 1:2], logits, 0.0), axis=1, keepdims=True)
            gate_ref[...] = jnp.where(live[:, 0:1], jax.nn.sigmoid(pick_a - pick_b), 0.0) + jnp.where(
                live[:, 1:2], jax.nn.sigmoid(pick_b - pick_a), 0.0
            )
        if slot == 3:
            plane1()

    back_step(1)
    ring_wait(6)
    ring_wait(7)
    expert([(zmod(z + 4), 0), (zmod(z + 4), 1)])
    back_step(2)
    back_step(3)
    plane2()
    for step in range(4, len(BACK)):
        back_step(step)
        if step == 6:
            plane3()

    for half in (1, 0):
        for way in range(2):
            landed(piece(sums.at[way], 0, half), back_recv.at[way, half, 0, 0])
        for pair in PAIRS[half]:
            at_rows = slice(pair * PAIR, (pair + 1) * PAIR)
            total = (
                partial[z, at_rows].astype(F32) + sums[0, 0, at_rows].astype(F32) + sums[1, 0, at_rows].astype(F32)
            ).astype(BF16)
            returning[:, :, pair * eighth:(pair + 1) * eighth] = spread(total)
        exchange(returning, returned, ret_send, ret_recv, half)
        own_back[half].start()
    plane4(0)
    gate = gate_ref[...]
    for half in (1, 0):
        put = one_hot(
            lax.broadcasted_iota(jnp.int32, (rows, SIZE[half]), 1) + START[half] == spot_ref[...]
        )
        own_back[half].wait()
        exchanged(returned, ret_recv, half)
        for i, pair in enumerate(PAIRS[half]):
            back_rows[half, i * PAIR:(i + 1) * PAIR, :] = gathered(returned, pair).astype(BF16)
        for j in range(width // 256):
            cols = slice(j * 256, (j + 1) * 256)
            got = jnp.dot(put, back_rows[half, :SIZE[half], cols], preferred_element_type=F32)
            before = hid[:, cols].astype(F32) if half else mixed[:, cols]
            mixed[:, cols] = before + got * gate

    def norm_out(i, carry):
        for j in range(4):
            at_rows = pl.ds(pl.multiple_of(i * 64 + j * 16, 16), 16)
            normed[at_rows, :] = norm_rows(mixed[at_rows, :], final_gain[...]).astype(BF16)
        return carry

    lax.fori_loop(0, rows // 64, norm_out, 0)
    plane4(1)

    groups = hw // 256

    def weight_cols(w, j):
        return weights[w, :, :, :, j * 256:(j + 1) * 256].reshape(width, 256)

    def kv_copy(j):
        return pltpu.make_async_remote_copy(
            src_ref=kv_out.at[j], dst_ref=kv_in.at[j], send_sem=kv_send.at[j], recv_sem=kv_recv.at[j],
            device_id={"grp": 1 - grp}, device_id_type=pl.DeviceIdType.MESH,
        )

    @pl.when(grp == 0)
    def _():
        for j in range(groups):
            for w in range(2):
                kv_out[j, w] = jnp.dot(
                    normed[...], weight_cols(w, j), preferred_element_type=F32
                ).astype(BF16)
            kv_copy(j).start()
        out_ref[...] = normed[...]
        for j in range(groups):
            kv_copy(j).wait_send()

    @pl.when(grp == 1)
    def _():
        for j in range(groups):
            query[j] = jnp.dot(
                normed[:ROWS_Q, :], weight_cols(0, j), preferred_element_type=F32
            ).astype(BF16)
        out_ref[ROWS_Q:, :] = mixed[ROWS_Q:, :].astype(BF16)

        q_pos = lax.broadcasted_iota(jnp.int32, (ROWS_Q, 1), 0)
        k_pos = lax.broadcasted_iota(jnp.int32, (1, rows), 1)
        seg_q = jnp.zeros((ROWS_Q, 1), jnp.int32)
        seg_k = jnp.zeros((1, rows), jnp.int32)
        q_end = jnp.zeros((1, 1), jnp.int32)
        k_end = jnp.zeros((1, 1), jnp.int32)
        for i in range(SENT):
            q_end = q_end + tgt_ref[:, i:i + 1]
            k_end = k_end + src_ref[:, i:i + 1]
            seg_q = seg_q + jnp.where(q_pos >= q_end, 1, 0)
            seg_k = seg_k + jnp.where(k_pos >= k_end, 1, 0)
        valid = seg_q < SENT
        allowed = (seg_q == seg_k) & valid
        for h in range(hw // HD):
            j, cols = h // 2, slice(h % 2 * HD, (h % 2 + 1) * HD)
            if h % 2 == 0:
                kv_copy(j).wait_recv()
            scores = lax.dot_general(
                query[j, :, cols], kv_in[j, 0, :, cols], (((1,), (1,)), ((), ())), preferred_element_type=F32
            ) * HD ** (-0.5)
            scores = jnp.where(allowed, scores, -1e30)
            top = jnp.max(scores, axis=-1, keepdims=True)
            expd = jnp.exp(scores - top)
            prob = (expd / jnp.sum(expd, axis=-1, keepdims=True)).astype(BF16)
            context[:, h * HD:(h + 1) * HD] = jnp.dot(
                prob, kv_in[j, 1, :, cols], preferred_element_type=F32
            ).astype(BF16)
        for j in range(width // 256):
            cols = slice(j * 256, (j + 1) * 256)
            wo_rows = weights[1, j * 2:(j + 1) * 2].reshape(256, hw)
            attended = lax.dot_general(
                context[...], wo_rows, (((1,), (1,)), ((), ())), preferred_element_type=F32
            )
            attended = jnp.where(valid, attended, 0.0)
            out_ref[:ROWS_Q, cols] = (mixed[:ROWS_Q, cols] + attended).astype(BF16)

    for copy in sent:
        copy.wait_send()


def body(
    hidden, norm_gain, final_gain, router, w_in, w_out, expert_ids, slot_ids, src_len, tgt_len, wq, wk, wv, wo,
):
    rows, width = hidden.shape[1:]
    hw = wq.shape[1]
    ff = w_in.shape[2]
    vmem = pl.BlockSpec(memory_space=pltpu.VMEM)
    anywhere = pl.BlockSpec(memory_space=pl.ANY)
    dma = pltpu.SemaphoreType.DMA
    out = pl.pallas_call(
        kernel,
        out_shape=pltpu.VMEM((rows, width), BF16),
        in_specs=[anywhere, vmem, vmem, anywhere, anywhere, anywhere] + [vmem] * 4 + [anywhere] * 4,
        out_specs=vmem,
        scratch_shapes=[
            pltpu.VMEM((rows, width), BF16),
            pltpu.VMEM((rows, width), BF16),
            pltpu.VMEM((width, 128), BF16),
            pltpu.VMEM((width, ff), BF16),
            pltpu.VMEM((ff, width), BF16),
            pltpu.VMEM((E, 16, 3 * width // 8), BF16),
            pltpu.VMEM((E, 16, 3 * width // 8), BF16),
            pltpu.VMEM((NZ, E * C, width), BF16),
            pltpu.VMEM((NZ, E * C, width), BF16),
            pltpu.VMEM((2, 4, E * C, width), BF16),
            pltpu.VMEM((4 * PAIR, ff), BF16),
            pltpu.VMEM((E, 16, 3 * width // 8), BF16),
            pltpu.VMEM((E, 16, 3 * width // 8), BF16),
            pltpu.VMEM((rows, width), F32),
            pltpu.VMEM((2, E, NZ, 16, hw), BF16),
            pltpu.VMEM((hw // 256, 2, rows, 256), BF16),
            pltpu.VMEM((hw // 256, 2, rows, 256), BF16),
            pltpu.VMEM((hw // 256, ROWS_Q, 256), BF16),
            pltpu.VMEM((ROWS_Q, hw), BF16),
            pltpu.VMEM((rows, 1), F32),
            pltpu.VMEM((rows, 1), jnp.int32),
            pltpu.VMEM((E * C, rows), BF16),
            pltpu.VMEM((E * 16, E * 16), BF16),
            pltpu.VMEM((E * 16, E * 16), BF16),
            pltpu.VMEM((2, 2 * PAIR, width), BF16),
            dma((10,)),
            dma((2, 15)),
            dma((2, E)),
            dma((2, 8)),
            dma((2, 8)),
            dma((2, len(BACK))),
            dma((2, 2, 4, 2)),
            dma((2, 2, 4)),
            dma((2, 2, 4)),
            dma((40,)),
            dma((2, E, 2)),
            dma((2, 15)),
            dma((2, E)),
            dma((hw // 256,)),
            dma((hw // 256,)),
        ],
        compiler_params=pltpu.CompilerParams(
            collective_id=0, has_side_effects=True, vmem_limit_bytes=56 * 1024 * 1024
        ),
        cost_estimate=pl.CostEstimate(flops=10**10, bytes_accessed=12 * 10**6, transcendentals=10**6),
    )(
        hidden[0], norm_gain, final_gain, router[0], w_in[0], w_out[0], expert_ids[0].T, slot_ids[0].T,
        src_len, tgt_len, wq, wk, wv, wo,
    )
    return out[None]


def solution(mesh):
    in_specs = (
        P("grp", "ep", None),
        P("grp", None),
        P("grp", None),
        P("grp", None, None),
        P("grp", None, "ep"),
        P("grp", "ep", None),
        P("grp", "ep", None),
        P("grp", "ep", None),
        P("ep", None),
        P("ep", None),
        P("ep", None),
        P("ep", None),
        P("ep", None),
        P("ep", None),
    )
    out_specs = P("grp", "ep", None)
    return jax.shard_map(body, mesh=mesh, in_specs=in_specs, out_specs=out_specs, check_vma=False)
```

```python
import jax
import jax.numpy as jnp
from jax import lax
from jax.experimental import pallas as pl
from jax.experimental.pallas import tpu as pltpu
from jax.sharding import PartitionSpec as P

NY, NX, NZ = 4, 4, 8
E = NY * NX
C = 6
PAIR = 2 * E
START = (0, PAIR)
SIZE = (PAIR, 2 * PAIR)
PAIRS = ((0,), (1, 2))
SENT = 4
HD = 128
ROWS_Q = 176
F32 = jnp.float32
BF16 = jnp.bfloat16

RING = [(0, 1), (1, 1), (0, 2), (1, 2), (0, 3), (1, 3), (0, 4), (1, 4)]
BACK = [
    (0, 3, "near"), (1, 3, "near"), (1, 4, "far"), (0, 4, "far"), (1, 3, "far"), (0, 3, "far"),
    (1, 2, "all"), (0, 2, "all"), (1, 1, "all"), (0, 1, "all"),
]


def norm_rows(v, gain):
    mean = jnp.mean(v, -1, keepdims=True)
    centred = v - mean
    spread = jnp.mean(centred * centred, -1, keepdims=True)
    return centred * lax.rsqrt(spread + 1e-05) * gain


def one_hot(hit):
    return hit.astype(F32).astype(BF16)


def kernel(
    hidden_hbm, norm_gain, final_gain, router_hbm, w_in_hbm, w_out_hbm, ids_ref, slots_ref, src_ref, tgt_ref,
    wq_hbm, wk_hbm, wv_hbm, wo_hbm,
    out_ref,
    hid, normed, router, w_in, w_out, packed, arrived, tokens, partial, sums, inner, returning, returned,
    mixed, weights, kv_out, kv_in, query, context, gate_ref, spot_ref, pick, perm, perm_t, back_rows,
    load_sem, pack_send, pack_recv, ring_send, ring_recv, back_send, back_recv, wz_send, wz_recv,
    wxy_send, wxy_recv, ret_send, ret_recv, kv_send, kv_recv,
):
    rows, width = hid.shape
    hw = width // 2
    eighth = width // 8
    ep = lax.axis_index("ep")
    grp = lax.axis_index("grp")
    z = lax.rem(ep, NZ)
    e = ep // NZ
    x = lax.rem(e, NX)
    y = e // NX

    def at(yy, xx, zz):
        return (yy * NX + xx) * NZ + zz

    def zmod(v):
        return lax.rem(v + NZ, NZ)

    def xmod(v):
        return lax.rem(v + NX, NX)

    def remote(src, dst, send, recv, target):
        return pltpu.make_async_remote_copy(
            src_ref=src, dst_ref=dst, send_sem=send, recv_sem=recv,
            device_id={"ep": target}, device_id_type=pl.DeviceIdType.MESH,
        )

    sent = []

    def send(*args):
        copy = remote(*args)
        copy.start()
        sent.append(copy)

    def landed(dst, recv):
        remote(dst, dst, kv_send.at[0], recv, ep).wait_recv()

    z_up, z_down = at(y, x, zmod(z + 1)), at(y, x, zmod(z - 1))
    peers = []
    for dy in (2, 1, 3, 0):
        for dx in (2, 1, 3, 0):
            if dy or dx:
                peers.append((xmod(y + dy), xmod(x + dx)))

    load_hidden = pltpu.make_async_copy(hidden_hbm, hid, load_sem.at[0])
    load_router = pltpu.make_async_copy(router_hbm, router, load_sem.at[1])
    load_in = pltpu.make_async_copy(w_in_hbm, w_in, load_sem.at[2])
    load_out = pltpu.make_async_copy(w_out_hbm, w_out, load_sem.at[3])

    def load_rows(w, source):
        return pltpu.make_async_copy(source, weights.at[w, e, z], load_sem.at[4 + w])

    load_hidden.start()

    @pl.when(grp == 0)
    def _():
        load_rows(0, wk_hbm).start()
        load_rows(1, wv_hbm).start()

    @pl.when(grp == 1)
    def _():
        load_rows(0, wq_hbm).start()
        load_rows(1, wo_hbm).start()

    barrier = pltpu.get_barrier_semaphore()
    for target in [at(yy, xx, z) for yy, xx in peers] + [at(y, x, zmod(z + k)) for k in (-2, -1, 1, 2)]:
        pl.semaphore_signal(barrier, inc=1, device_id={"ep": target}, device_id_type=pl.DeviceIdType.MESH)
    pl.semaphore_signal(barrier, inc=1, device_id={"grp": 1 - grp}, device_id_type=pl.DeviceIdType.MESH)
    load_router.start()
    load_in.start()
    load_out.start()

    ids_row = ids_ref[...]
    slots_row = slots_ref[...]
    pair_row = jnp.where(slots_row >= 2, 1, 0) + jnp.where(slots_row >= 4, 1, 0)
    spot = jnp.where(slots_row >= 0, pair_row * (PAIR - 2) + 2 * ids_row + slots_row, -1000)
    spot = jnp.max(spot, axis=0, keepdims=True)
    stacked = jnp.concatenate([ids_row, slots_row] + [spot] * 4, axis=0)
    columns = jnp.transpose(stacked.astype(F32)).astype(jnp.int32)
    ids, live, spot_ref[...] = columns[:, 0:2], columns[:, 2:4] >= 0, columns[:, 4:5]
    pick[...] = one_hot(lax.broadcasted_iota(jnp.int32, (E * C, rows), 0) == spot)
    i_iota = lax.broadcasted_iota(jnp.int32, (E * 16, E * 16), 0)
    j_iota = lax.broadcasted_iota(jnp.int32, (E * 16, E * 16), 1)
    perm[...] = one_hot(j_iota == (i_iota % 16) // 2 * PAIR + i_iota // 16 * 2 + i_iota % 2)
    perm_t[...] = one_hot(i_iota == (j_iota % 16) // 2 * PAIR + j_iota // 16 * 2 + j_iota % 2)

    pl.semaphore_wait(barrier, len(peers) + 5)
    load_rows(0, wq_hbm).wait()
    load_rows(1, wq_hbm).wait()

    def ways():
        return enumerate(((1, z_up), (-1, z_down)))

    def part(ref, way, k):
        if k < 4:
            return ref
        size = ref.shape[-1] // 2
        return ref.at[:, pl.ds(way * size, size)]

    def wz_send_rows(w, block, way, reach, dist):
        ref = part(weights.at[w, e, block], way, dist)
        target = at(y, x, zmod(z + (reach, -reach)[way]))
        send(ref, ref, wz_send.at[w, way, dist - 1], wz_recv.at[w, way, dist - 1], target)

    def wz_wait(w, way, dist):
        block = zmod(z - (dist, -dist)[way])
        landed(part(weights.at[w, e, block], way, dist), wz_recv.at[w, way, dist - 1])

    def wz_near():
        for dist in (2, 1):
            for w in range(2):
                for way in range(2):
                    wz_send_rows(w, z, way, dist, dist)

    def wz_far():
        for w in range(2):
            for way in range(2):
                wz_wait(w, way, 2)
                block = zmod(z - (2, -2)[way])
                wz_send_rows(w, block, way, 1, 3)
                wz_send_rows(w, block, way, 2, 4)

    def wz_end():
        for w in range(2):
            for way in range(2):
                for dist in (1, 3, 4):
                    wz_wait(w, way, dist)

    wz_near()

    load_hidden.wait()

    def norm_in(i, carry):
        for j in range(4):
            at_rows = pl.ds(pl.multiple_of(i * 64 + j * 16, 16), 16)
            normed[at_rows, :] = norm_rows(hid[at_rows, :].astype(F32), norm_gain[...]).astype(BF16)
        return carry

    def spread(pair_rows):
        tall = jnp.concatenate([pair_rows[:, q * eighth:(q + 1) * eighth] for q in range(8)], axis=0)
        return jnp.dot(perm[...], tall, preferred_element_type=F32).astype(BF16).reshape(E, 16, eighth)

    def gathered(ref, pair):
        tall = jnp.dot(
            perm_t[...], ref[:, :, pair * eighth:(pair + 1) * eighth].reshape(E * 16, eighth),
            preferred_element_type=F32,
        )
        return jnp.concatenate([tall[q * PAIR:(q + 1) * PAIR] for q in range(8)], axis=1)

    def piece(ref, block, half):
        return ref.at[block, pl.ds(START[half], SIZE[half])]

    def exchange(source, target, send_sem, recv_sem, half):
        for i, (yy, xx) in enumerate(peers):
            peer = yy * NX + xx
            send(
                pair_cols_at(source, peer, half), pair_cols_at(target, e, half), send_sem.at[half, i],
                recv_sem.at[half, e], peer * NZ + z,
            )

    def pair_cols_at(ref, block, half):
        return ref.at[block, :, pl.ds(PAIRS[half][0] * eighth, len(PAIRS[half]) * eighth)]

    def exchanged(target, recv_sem, half):
        for yy, xx in peers:
            peer = yy * NX + xx
            landed(pair_cols_at(target, peer, half), recv_sem.at[half, peer])

    own_slots = [
        pltpu.make_async_copy(pair_cols_at(packed, e, h), pair_cols_at(arrived, e, h), load_sem.at[6 + h])
        for h in range(2)
    ]
    own_back = [
        pltpu.make_async_copy(pair_cols_at(returning, e, h), pair_cols_at(returned, e, h), load_sem.at[8 + h])
        for h in range(2)
    ]
    for half in range(2):
        picked = jnp.dot(
            pick[START[half]:START[half] + SIZE[half], :], hid[...], preferred_element_type=F32
        ).astype(BF16)
        for i, pair in enumerate(PAIRS[half]):
            packed[:, :, pair * eighth:(pair + 1) * eighth] = spread(picked[i * PAIR:(i + 1) * PAIR])
        exchange(packed, arrived, pack_send, pack_recv, half)
        own_slots[half].start()

    def slots_in(half):
        own_slots[half].wait()
        exchanged(arrived, pack_recv, half)
        for pair in PAIRS[half]:
            tokens[z, pair * PAIR:(pair + 1) * PAIR, :] = norm_rows(
                gathered(arrived, pair), norm_gain[...]
            ).astype(BF16)

    def ring_hop(slot):
        half, k = RING[slot]
        for way, (sign, target) in ways():
            ref = part(piece(tokens, zmod(z - sign * (k - 1)), half), way, k)
            send(ref, ref, ring_send.at[way, slot], ring_recv.at[way, slot], target)

    def ring_wait(slot):
        half, k = RING[slot]
        for way, (sign, _) in ways():
            landed(part(piece(tokens, zmod(z - sign * k), half), way, k), ring_recv.at[way, slot])

    def expert(parts):
        count = sum(SIZE[half] for _, half in parts)

        def first_step(j, carry):
            cols = pl.ds(pl.multiple_of(j * 256, 256), 256)
            blocks = [tokens[block, START[half]:START[half] + SIZE[half]] for block, half in parts]
            both = jnp.concatenate(blocks, axis=0)
            got = jnp.dot(both, w_in[:, cols], preferred_element_type=F32)
            inner[:count, cols] = jnp.maximum(got, 0.0).astype(BF16)
            return carry

        def second_step(j, carry):
            cols = pl.ds(pl.multiple_of(j * 256, 256), 256)
            got = jnp.dot(inner[:count, :], w_out[:, cols], preferred_element_type=F32).astype(BF16)
            row = 0
            for block, half in parts:
                partial[block, START[half]:START[half] + SIZE[half], cols] = got[row:row + SIZE[half]]
                row += SIZE[half]
            return carry

        lax.fori_loop(0, w_in.shape[1] // 256, first_step, 0, unroll=True)
        lax.fori_loop(0, width // 256, second_step, 0, unroll=True)

    def expert_slot(slot):
        half, k = RING[slot]
        expert([(zmod(z - k), half), (zmod(z + k), half)] if k < 4 else [(zmod(z + k), half)])

    def block_at(w, a, b):
        xx, yy = (xmod(x + a), xmod(y + b)) if w == 0 else (xmod(x + b), xmod(y + a))
        return yy * NX + xx

    def go(w, phase, sign):
        if (w == 0) == (phase == 0):
            return at(y, xmod(x + sign), z)
        return at(xmod(y + sign), x, z)

    w_count = [0]

    def wxy(w, a, b, piece, phase, sign):
        blk = block_at(w, a, b)
        ref = weights.at[w, blk] if piece is None else weights.at[w, blk, pl.ds(piece * 4, 4)]
        send(ref, ref, wxy_send.at[w_count[0]], wxy_recv.at[w, blk, piece or 0], go(w, phase, sign))
        w_count[0] += 1

    def wxy_wait(w, a, b):
        blk = block_at(w, a, b)
        opposite = b == 2 or (b == 0 and a == 2)
        if opposite:
            for piece in range(2):
                landed(weights.at[w, blk, pl.ds(piece * 4, 4)], wxy_recv.at[w, blk, piece])
        else:
            landed(weights.at[w, blk], wxy_recv.at[w, blk, 0])

    def forward(w, a, b, phase):
        if phase == 0:
            wxy(w, a, b, 0 if a == 1 else 1, 0, -1 if a == 1 else 1)
        else:
            wxy(w, a, b, 0 if b == 1 else 1, 1, -1 if b == 1 else 1)

    def plane0():
        for w in range(2):
            for phase in range(2):
                for sign in (1, -1):
                    wxy(w, 0, 0, None, phase, sign)

    def plane1():
        for w in range(2):
            for a in (1, 3):
                wxy_wait(w, a, 0)
                forward(w, a, 0, 0)
        for w in range(2):
            for b in (1, 3):
                wxy_wait(w, 0, b)
                forward(w, 0, b, 1)
        for w in range(2):
            for a in (1, 3):
                for sign in (1, -1):
                    wxy(w, a, 0, None, 1, sign)

    def plane2():
        for w in range(2):
            wxy_wait(w, 2, 0)
            for sign in (1, -1):
                wxy(w, 2, 0, None, 1, sign)
        for w in range(2):
            for a in (1, 3):
                for b in (1, 3):
                    wxy_wait(w, a, b)
                    forward(w, a, b, 1)

    def plane3():
        for w in range(2):
            for b in (1, 3):
                wxy_wait(w, 2, b)
                forward(w, 2, b, 1)

    def plane4(w):
        for a in range(4):
            wxy_wait(w, a, 2)

    wz_far()
    def columns_of(ref, way, kind):
        if kind == "all":
            return ref
        size = ref.shape[-1] // 2
        return ref.at[:, pl.ds((way if kind == "far" else 1 - way) * size, size)]

    def back_step(step):
        half, k, kind = BACK[step]
        for way, (sign, target) in enumerate(((1, z_down), (-1, z_up))):
            here = columns_of(piece(partial, zmod(z - sign * k), half), way, kind)
            came = columns_of(piece(sums.at[way], min(k, 3), half), way, kind)
            if k == 2:
                for i, other in enumerate(("far", "near")):
                    landed(columns_of(piece(sums.at[way], 2, half), way, other), back_recv.at[way, half, 2, i])
            elif k == 1 or (k == 3 and kind == "far"):
                landed(came, back_recv.at[way, half, k, 0])
            if k < 3 or (k == 3 and kind == "far"):
                here[...] = (here[...].astype(F32) + came[...].astype(F32)).astype(BF16)
            send(
                here, columns_of(piece(sums.at[way], k - 1, half), way, kind), back_send.at[way, step],
                back_recv.at[way, half, k - 1, 1 if kind == "near" else 0], target,
            )

    slots_in(0)
    ring_hop(0)
    slots_in(1)
    ring_hop(1)
    load_in.wait()
    load_out.wait()
    wz_end()
    plane0()
    expert([(z, 0), (z, 1)])
    for slot in range(6):
        ring_wait(slot)
        ring_hop(slot + 2)
        if slot == 5:
            back_step(0)
        expert_slot(slot)
        if slot == 1:
            load_router.wait()
            lax.fori_loop(0, rows // 64, norm_in, 0)
            logits = jnp.dot(normed[...], router[...], preferred_element_type=F32)
            lane = lax.broadcasted_iota(jnp.int32, logits.shape, 1)
            pick_a = jnp.sum(jnp.where(lane == ids[:, 0:1], logits, 0.0), axis=1, keepdims=True)
            pick_b = jnp.sum(jnp.where(lane == ids[:, 1:2], logits, 0.0), axis=1, keepdims=True)
            gate_ref[...] = jnp.where(live[:, 0:1], jax.nn.sigmoid(pick_a - pick_b), 0.0) + jnp.where(
                live[:, 1:2], jax.nn.sigmoid(pick_b - pick_a), 0.0
            )
        if slot == 3:
            plane1()

    back_step(1)
    ring_wait(6)
    ring_wait(7)
    expert([(zmod(z + 4), 0), (zmod(z + 4), 1)])
    back_step(2)
    back_step(3)
    plane2()
    for step in range(4, len(BACK)):
        back_step(step)
        if step == 6:
            plane3()

    for half in (1, 0):
        for way in range(2):
            landed(piece(sums.at[way], 0, half), back_recv.at[way, half, 0, 0])
        for pair in PAIRS[half]:
            at_rows = slice(pair * PAIR, (pair + 1) * PAIR)
            total = (
                partial[z, at_rows].astype(F32) + sums[0, 0, at_rows].astype(F32) + sums[1, 0, at_rows].astype(F32)
            ).astype(BF16)
            returning[:, :, pair * eighth:(pair + 1) * eighth] = spread(total)
        exchange(returning, returned, ret_send, ret_recv, half)
        own_back[half].start()
    plane4(0)
    gate = gate_ref[...]
    for half in (1, 0):
        put = one_hot(
            lax.broadcasted_iota(jnp.int32, (rows, SIZE[half]), 1) + START[half] == spot_ref[...]
        )
        own_back[half].wait()
        exchanged(returned, ret_recv, half)
        for i, pair in enumerate(PAIRS[half]):
            back_rows[half, i * PAIR:(i + 1) * PAIR, :] = gathered(returned, pair).astype(BF16)
        for j in range(width // 256):
            cols = slice(j * 256, (j + 1) * 256)
            got = jnp.dot(put, back_rows[half, :SIZE[half], cols], preferred_element_type=F32)
            before = hid[:, cols].astype(F32) if half else mixed[:, cols]
            mixed[:, cols] = before + got * gate

    def norm_out(i, carry):
        for j in range(4):
            at_rows = pl.ds(pl.multiple_of(i * 64 + j * 16, 16), 16)
            normed[at_rows, :] = norm_rows(mixed[at_rows, :], final_gain[...]).astype(BF16)
        return carry

    lax.fori_loop(0, rows // 64, norm_out, 0, unroll=True)
    plane4(1)

    groups = hw // 256

    def weight_cols(w, j):
        return weights[w, :, :, :, j * 256:(j + 1) * 256].reshape(width, 256)

    def kv_copy(j):
        return pltpu.make_async_remote_copy(
            src_ref=kv_out.at[j], dst_ref=kv_in.at[j], send_sem=kv_send.at[j], recv_sem=kv_recv.at[j],
            device_id={"grp": 1 - grp}, device_id_type=pl.DeviceIdType.MESH,
        )

    @pl.when(grp == 0)
    def _():
        for j in range(groups):
            for w in range(2):
                kv_out[j, w] = jnp.dot(
                    normed[...], weight_cols(w, j), preferred_element_type=F32
                ).astype(BF16)
            kv_copy(j).start()
        out_ref[...] = normed[...]
        for j in range(groups):
            kv_copy(j).wait_send()

    @pl.when(grp == 1)
    def _():
        for j in range(groups):
            query[j] = jnp.dot(
                normed[:ROWS_Q, :], weight_cols(0, j), preferred_element_type=F32
            ).astype(BF16)
        out_ref[ROWS_Q:, :] = mixed[ROWS_Q:, :].astype(BF16)

        q_pos = lax.broadcasted_iota(jnp.int32, (ROWS_Q, 1), 0)
        k_pos = lax.broadcasted_iota(jnp.int32, (1, rows), 1)
        seg_q = jnp.zeros((ROWS_Q, 1), jnp.int32)
        seg_k = jnp.zeros((1, rows), jnp.int32)
        q_end = jnp.zeros((1, 1), jnp.int32)
        k_end = jnp.zeros((1, 1), jnp.int32)
        for i in range(SENT):
            q_end = q_end + tgt_ref[:, i:i + 1]
            k_end = k_end + src_ref[:, i:i + 1]
            seg_q = seg_q + jnp.where(q_pos >= q_end, 1, 0)
            seg_k = seg_k + jnp.where(k_pos >= k_end, 1, 0)
        valid = seg_q < SENT
        allowed = (seg_q == seg_k) & valid
        for h in range(hw // HD):
            j, cols = h // 2, slice(h % 2 * HD, (h % 2 + 1) * HD)
            if h % 2 == 0:
                kv_copy(j).wait_recv()
            scores = lax.dot_general(
                query[j, :, cols], kv_in[j, 0, :, cols], (((1,), (1,)), ((), ())), preferred_element_type=F32
            ) * HD ** (-0.5)
            scores = jnp.where(allowed, scores, -1e30)
            top = jnp.max(scores, axis=-1, keepdims=True)
            expd = jnp.exp(scores - top)
            prob = (expd / jnp.sum(expd, axis=-1, keepdims=True)).astype(BF16)
            context[:, h * HD:(h + 1) * HD] = jnp.dot(
                prob, kv_in[j, 1, :, cols], preferred_element_type=F32
            ).astype(BF16)
        for j in range(width // 256):
            cols = slice(j * 256, (j + 1) * 256)
            wo_rows = weights[1, j * 2:(j + 1) * 2].reshape(256, hw)
            attended = lax.dot_general(
                context[...], wo_rows, (((1,), (1,)), ((), ())), preferred_element_type=F32
            )
            attended = jnp.where(valid, attended, 0.0)
            out_ref[:ROWS_Q, cols] = (mixed[:ROWS_Q, cols] + attended).astype(BF16)

    for copy in sent:
        copy.wait_send()


def body(
    hidden, norm_gain, final_gain, router, w_in, w_out, expert_ids, slot_ids, src_len, tgt_len, wq, wk, wv, wo,
):
    rows, width = hidden.shape[1:]
    hw = wq.shape[1]
    ff = w_in.shape[2]
    vmem = pl.BlockSpec(memory_space=pltpu.VMEM)
    anywhere = pl.BlockSpec(memory_space=pl.ANY)
    dma = pltpu.SemaphoreType.DMA
    out = pl.pallas_call(
        kernel,
        out_shape=pltpu.VMEM((rows, width), BF16),
        in_specs=[anywhere, vmem, vmem, anywhere, anywhere, anywhere] + [vmem] * 4 + [anywhere] * 4,
        out_specs=vmem,
        scratch_shapes=[
            pltpu.VMEM((rows, width), BF16),
            pltpu.VMEM((rows, width), BF16),
            pltpu.VMEM((width, 128), BF16),
            pltpu.VMEM((width, ff), BF16),
            pltpu.VMEM((ff, width), BF16),
            pltpu.VMEM((E, 16, 3 * width // 8), BF16),
            pltpu.VMEM((E, 16, 3 * width // 8), BF16),
            pltpu.VMEM((NZ, E * C, width), BF16),
            pltpu.VMEM((NZ, E * C, width), BF16),
            pltpu.VMEM((2, 4, E * C, width), BF16),
            pltpu.VMEM((4 * PAIR, ff), BF16),
            pltpu.VMEM((E, 16, 3 * width // 8), BF16),
            pltpu.VMEM((E, 16, 3 * width // 8), BF16),
            pltpu.VMEM((rows, width), F32),
            pltpu.VMEM((2, E, NZ, 16, hw), BF16),
            pltpu.VMEM((hw // 256, 2, rows, 256), BF16),
            pltpu.VMEM((hw // 256, 2, rows, 256), BF16),
            pltpu.VMEM((hw // 256, ROWS_Q, 256), BF16),
            pltpu.VMEM((ROWS_Q, hw), BF16),
            pltpu.VMEM((rows, 1), F32),
            pltpu.VMEM((rows, 1), jnp.int32),
            pltpu.VMEM((E * C, rows), BF16),
            pltpu.VMEM((E * 16, E * 16), BF16),
            pltpu.VMEM((E * 16, E * 16), BF16),
            pltpu.VMEM((2, 2 * PAIR, width), BF16),
            dma((10,)),
            dma((2, 15)),
            dma((2, E)),
            dma((2, 8)),
            dma((2, 8)),
            dma((2, len(BACK))),
            dma((2, 2, 4, 2)),
            dma((2, 2, 4)),
            dma((2, 2, 4)),
            dma((40,)),
            dma((2, E, 2)),
            dma((2, 15)),
            dma((2, E)),
            dma((hw // 256,)),
            dma((hw // 256,)),
        ],
        compiler_params=pltpu.CompilerParams(
            collective_id=0, has_side_effects=True, vmem_limit_bytes=56 * 1024 * 1024
        ),
        cost_estimate=pl.CostEstimate(flops=10**10, bytes_accessed=12 * 10**6, transcendentals=10**6),
    )(
        hidden[0], norm_gain, final_gain, router[0], w_in[0], w_out[0], expert_ids[0].T, slot_ids[0].T,
        src_len, tgt_len, wq, wk, wv, wo,
    )
    return out[None]


def solution(mesh):
    in_specs = (
        P("grp", "ep", None),
        P("grp", None),
        P("grp", None),
        P("grp", None, None),
        P("grp", None, "ep"),
        P("grp", "ep", None),
        P("grp", "ep", None),
        P("grp", "ep", None),
        P("ep", None),
        P("ep", None),
        P("ep", None),
        P("ep", None),
        P("ep", None),
        P("ep", None),
    )
    out_specs = P("grp", "ep", None)
    return jax.shard_map(body, mesh=mesh, in_specs=in_specs, out_specs=out_specs, check_vma=False)
```
